256 devices in a mesh: row: 8 (over x, core), col: 32 (over z, y).
Axes of the slice: x: 4, y: 4, z: 8, core: 2. Of those that a mesh axis runs over, the one named last changes fastest.
Arguments:
- trailing_cot: bfloat16 [16, 2048, 4, 8192], P(None, 'row', None, 'col'), may hold values from -6 to 6
- panel_factor: bfloat16 [16, 2048, 256], P(None, ('row', 'col')), may hold values from -0.03125 to 0.03125
- panel_cot: bfloat16 [16, 2048, 256], P(None, ('row', 'col')), may hold values from -6 to 6
- block_inverse: float32 [256, 256], replicated, as said below
- row_desc: bfloat16 [16, 2048, 256], P(None, 'row'), may hold values from -6 to 6
- panel_desc: bfloat16 [256, 256], replicated, may hold values from -6 to 6
Outputs:
- adjoint: float32 [16, 2048, 256], P(None, ('row', 'col'))
- diag_cot: float32 [256, 256], replicated
- slope: float32 [2], replicated
The draws below stay inside these ranges and needn't reach their ends.
Inputs may be any that keep to these rules, and one draw needn't show every extreme that they name: `block_inverse`: lower triangular, diagonal between 0.6 and 1.4.
All inputs are finite; a program needn't handle non-finite values.
Results may differ from the reference program's by a relative error of at most 0.0003.
Values may be sent and summed in bfloat16 or wider, within the bound.
A program may use at most 128 MiB of HBM per device.

```python
import math
import jax
import jax.numpy as jnp
from jax import lax

TILE = 256
FEAT = 256
TROWS = 16
TCOLS = 4
ORDER = 32768
N_ROW = 8
N_COL = 32


def draw_block_inverse(key, part):
    key = jax.random.fold_in(key, 11)
    first, second = jax.random.split(key)
    diag_vals = jax.random.uniform(first, (TILE,), jnp.float32, 0.6, 1.4)
    lower = jax.random.normal(second, (TILE, TILE), jnp.float32) * (0.6 / TILE ** 0.5)
    return jnp.tril(lower, -1) + jnp.eye(TILE, dtype=jnp.float32) * diag_vals[None, :]


def raised(array, own_key, source, target, blocks, factor):
    owner, partner = [(jnp.arange(array.shape[dim]) // (array.shape[dim] // blocks)).reshape([-1 if axis == dim else 1 for axis in range(array.ndim)]) for dim in (source, target)]
    chosen = jax.random.permutation(own_key, blocks)[partner]
    strong = (owner == chosen) | (owner == (partner + blocks // 2) % blocks)
    return jnp.where(strong, factor * array, array)


def block_scale(key, shape, pieces, smallest, high):
    loudness, own = 1.0, jax.random.fold_in(key, 6)
    for position, blocks in pieces:
        steps = jnp.exp(jax.random.uniform(jax.random.fold_in(own, position), (blocks,), jnp.float32, smallest / len(pieces), high / len(pieces)))
        loudness = loudness * jnp.repeat(steps, shape[position] // blocks).reshape([-1 if axis == position else 1 for axis in range(len(shape))])
    return loudness


def centred(own_key, dims, deviation, limit, shards=(), kind=jnp.bfloat16):
    values = deviation * jax.random.normal(own_key, dims, jnp.float32)
    if shards:
        values = values * block_scale(own_key, dims, shards, -0.22, 0.18)
    return jnp.clip(values, -limit, limit).astype(kind)


def gaussian_with(rng, shape, scale, bound, shards, heavy, kind=jnp.bfloat16):
    result = scale * jax.random.normal(rng, shape, jnp.float32)
    if shards:
        result = result * block_scale(rng, shape, shards, -0.22, 0.18)
    return jnp.clip(raised(result, jax.random.fold_in(rng, 3), *heavy), -bound, bound).astype(kind)


def setup_inputs(seed: int = 0) -> dict:
    arg_keys = jax.random.split(jax.random.key(seed), 7)
    return {
        "trailing_cot": gaussian_with(arg_keys[0], (TROWS, N_ROW * TILE, TCOLS, N_COL * TILE), 1.0, 6.0, ((1, 8), (3, 32)), (3, 1, 32, 2.75)),
        "panel_factor": centred(arg_keys[1], (TROWS, N_ROW * TILE, TILE), ORDER ** -0.5, 0.03125, ((1, 256),)),
        "panel_cot": centred(arg_keys[2], (TROWS, N_ROW * TILE, TILE), 1.0, 6.0, ((1, 256),)),
        "block_inverse": draw_block_inverse(jax.random.fold_in(arg_keys[6], 71), 0),
        "row_desc": centred(arg_keys[4], (TROWS, N_ROW * TILE, FEAT), 1.0, 6.0, ((1, 8),)),
        "panel_desc": centred(arg_keys[5], (TILE, FEAT), 1.0, 6.0),
    }


def kernel_slope(left, right, left_norm, right_norm):
    cross = jnp.dot(left, right.T, preferred_element_type=jnp.float32)
    scaled = 2.0 * (left_norm[:, None] + right_norm[None, :] - 2.0 * cross) / FEAT
    return 2.0 * scaled * jnp.exp(-scaled)

def reference(trailing_cot, panel_factor, panel_cot, block_inverse, row_desc, panel_desc):
    order = TROWS * N_ROW * TILE
    factor = panel_factor.reshape(order, TILE)
    whole = trailing_cot.reshape(order, order)
    product = jnp.dot(whole, factor, preferred_element_type=jnp.float32)
    total = panel_cot.reshape(order, TILE).astype(jnp.float32) - 2.0 * product
    adjoint = jnp.dot(total, block_inverse, precision=lax.Precision.HIGHEST)
    moment = jnp.dot(total.T, factor.astype(jnp.float32), precision=lax.Precision.HIGHEST)
    diag_cot = -jnp.tril(jnp.dot(block_inverse.T, moment, precision=lax.Precision.HIGHEST))
    descs = row_desc.reshape(order, FEAT)
    norms = lax.optimization_barrier(jnp.sum(jnp.square(descs.astype(jnp.float32)), axis=-1))

    def block_term(items):
        rows, blk_desc, blk_norm = items
        return jnp.sum(rows.astype(jnp.float32) * kernel_slope(blk_desc, descs, blk_norm, norms))
    parts = lax.map(block_term, (whole.reshape(TROWS, N_ROW * TILE, order), descs.reshape(TROWS, N_ROW * TILE, FEAT), norms.reshape(TROWS, N_ROW * TILE)))
    trail = jnp.sum(parts) / order
    panel_norm = lax.optimization_barrier(jnp.sum(jnp.square(panel_desc.astype(jnp.float32)), axis=-1))
    panel_term = jnp.sum(adjoint * kernel_slope(descs, panel_desc, norms, panel_norm)) / math.sqrt(order * TILE)
    slope = jnp.stack([trail, panel_term]).astype(jnp.float32)
    return (adjoint.reshape(TROWS, N_ROW * TILE, TILE), diag_cot, slope)
```

```python
import functools
import math

import jax
import jax.numpy as jnp
from jax import lax
from jax.experimental import pallas as pl
from jax.experimental.pallas import tpu as pltpu
from jax.sharding import PartitionSpec as P

MESH = pl.DeviceIdType.MESH
HIGHEST = lax.Precision.HIGHEST
F32 = jnp.float32
BF16 = jnp.bfloat16
LOG2E = math.log2(math.e)

TR = 16
TC = 4
NX, NY, NZ, NR = 4, 4, 8, 8
PER = 2
KINDS = "ABABABAA"
N_A = KINDS.count("A")
N_B = KINDS.count("B")
STEPS = 7


def kernel(
    f_hbm, u_hbm, s_hbm, c_ref, f_own, b_ref, pd_ref,
    adj_ref, diag_ref, slope_ref,
    s_raw, s_f32, s_rel, u_row, u_col, norm_row, norm_col, f_buf, f_col, prod, total,
    ay1, ay2, az1, az2, bz1, bz2, by1, by2,
    m1, m1r, m2, m2r, m3, m4, m5,
    s_sem, u_sem, f_send, f_recv, f_local, ucol_send, ucol_recv, rs_send, rs_recv, m_send, m_recv,
):
    r = lax.axis_index("row")
    c = lax.axis_index("col")
    x, core = r // 2, r % 2
    z, y = c // NY, c % NY
    root = c % NR
    quarter = c // NR
    is_root = root == r

    barrier = pltpu.get_barrier_semaphore()

    def greet(dev):
        pl.semaphore_signal(barrier, inc=1, device_id=dev, device_id_type=MESH)

    @pl.loop(0, 16)
    def _(m):
        @pl.when(jnp.logical_not(jnp.logical_and(is_root, 2 * m + core == c)))
        def _():
            greet((root, 2 * m + core))

    @pl.loop(1, NR)
    def _(d):
        greet(((r + d) % NR, c))

    @pl.loop(1, NY)
    def _(d):
        greet((r, z * NY + (y + d) % NY))

    @pl.loop(1, NZ)
    def _(d):
        greet((r, ((z + d) % NZ) * NY + y))

    s_copies = [
        pltpu.make_async_copy(s_hbm.at[pl.ds(t * 2048, 2048)], s_raw.at[t], s_sem.at[t])
        for t in range(TR)
    ]
    u_copy = pltpu.make_async_copy(u_hbm, u_row, u_sem)
    for cp in s_copies[:2]:
        cp.start()
    u_copy.start()
    for cp in s_copies[2:]:
        cp.start()

    pl.semaphore_wait(barrier, 16 + 7 + 3 + 7 - jnp.where(is_root, 1, 0))

    @pl.loop(0, 16)
    def _(n):
        q, xd = n // NX, n % NX
        mine = jnp.logical_and(is_root, jnp.logical_and(q == quarter, xd == x))

        @pl.when(mine)
        def _():
            pltpu.make_async_copy(f_hbm.at[q], f_buf.at[c % 2, c // 2], f_recv.at[0]).start()

        @pl.when(jnp.logical_not(mine))
        def _():
            pltpu.make_async_remote_copy(
                src_ref=f_hbm.at[q], dst_ref=f_buf.at[c % 2, c // 2],
                send_sem=f_send.at[n], recv_sem=f_recv.at[0],
                device_id=(2 * xd + c % 2, NR * q + r), device_id_type=MESH,
            ).start()

    def ucol_to(d):
        return pltpu.make_async_remote_copy(
            src_ref=u_hbm.at[:, quarter], dst_ref=u_col,
            send_sem=ucol_send.at[d], recv_sem=ucol_recv,
            device_id=(((x + d) % NX) * 2 + core, c), device_id_type=MESH,
        )

    @pl.when(is_root)
    def _():
        for d in (1, 3, 2):
            ucol_to(d).start()
        pltpu.make_async_copy(u_hbm.at[:, quarter], u_col, ucol_recv).start()

    def relay(t):
        s_f32[...] = s_raw[t].astype(F32)
        for u in range(TC):
            for half in range(2):
                s_rel[t, u, :, half * 128 : half * 128 + 128] = s_f32[
                    pl.ds(half * 4 + u, 256, stride=8), :
                ].astype(BF16)

    for t in range(TR):
        s_copies[t].wait()

    @pl.loop(0, TR)
    def _(t):
        relay(t)

    u_copy.wait()

    @pl.loop(0, TR)
    def _(t):
        rows = u_row[t // 4, t % 4].astype(F32)
        norm = jnp.sum(rows * rows, axis=-1, keepdims=True) * (2.0 * LOG2E / 256.0)
        norm_row[t] = jnp.broadcast_to(norm, (256, 128))

    sibling = (2 * x + 1 - core, c)

    pltpu.make_async_copy(f_buf.at[0], f_buf.at[0], f_recv.at[0]).wait()
    f_swap = pltpu.make_async_remote_copy(
        src_ref=f_buf.at[core], dst_ref=f_buf.at[core],
        send_sem=f_local, recv_sem=f_recv.at[1],
        device_id=sibling, device_id_type=MESH,
    )
    f_swap.start()
    f_swap.wait_recv()

    @pl.loop(0, 16)
    def _(m):
        even = f_buf[0, m].astype(F32)
        odd = f_buf[1, m].astype(F32)
        for u in range(TC):
            rows = jnp.concatenate([even[8 * u : 8 * u + 8], odd[8 * u : 8 * u + 8]], axis=0)
            f_col[u, pl.ds(pl.multiple_of(m * 16, 16), 16), :] = rows.astype(BF16)

    neighbours = {
        "y": ((r, z * NY + (y + 1) % NY), (r, z * NY + (y + NY - 1) % NY)),
        "z": ((r, ((z + 1) % NZ) * NY + y), (r, ((z + NZ - 1) % NZ) * NY + y)),
    }
    size = {"y": NY, "z": NZ}
    here = {"y": y, "z": z}
    lanes = (pl.ds(0, 128), pl.ds(128, 128))
    full = pl.ds(0, 256)
    group_slot = {}
    for g, kind in enumerate(KINDS):
        group_slot[g] = KINDS[:g].count(kind)

    def part(g, axis, dest, lane):
        rows = pl.ds(g * PER, PER)
        if KINDS[g] == "A":
            if axis == "y":
                return (rows, slice(None), dest, slice(None), lane)
            return (rows, dest, y, slice(None), lane)
        if axis == "z":
            return (rows, dest, slice(None), slice(None), lane)
        return (rows, z, dest, slice(None), lane)

    def box(g, axis, rnd, way):
        slot = group_slot[g]
        if KINDS[g] == "A":
            first, later = (ay1, ay2) if axis == "y" else (az1, az2)
        else:
            first, later = (bz1, bz2) if axis == "z" else (by1, by2)
        if rnd == 0:
            return first.at[slot, way]
        return later.at[slot, way, rnd - 1]

    def sem_of(g, axis, rnd, way):
        second = axis == ("z" if KINDS[g] == "A" else "y")
        offset = (size["y"] // 2 if KINDS[g] == "A" else size["z"] // 2) if second else 0
        return (g * 6 + offset + rnd) * 2 + way

    def copy_of(g, axis, rnd, way):
        n = size[axis]
        reach = n // 2 - rnd
        sign = 1 if way == 0 else n - 1
        dest = (here[axis] + sign * reach) % n
        lane = lanes[way] if rnd == 0 else full
        k = sem_of(g, axis, rnd, way)
        return pltpu.make_async_remote_copy(
            src_ref=prod.at[part(g, axis, dest, lane)],
            dst_ref=box(g, axis, rnd, way),
            send_sem=rs_send.at[k], recv_sem=rs_recv.at[k],
            device_id=neighbours[axis][way], device_id_type=MESH,
        )

    def take(g, axis, rnd, way):
        n = size[axis]
        reach = n // 2 - rnd - 1
        sign = 1 if way == 0 else n - 1
        dest = (here[axis] + sign * reach) % n
        lane = lanes[way] if rnd == 0 else full
        copy_of(g, axis, rnd, way).wait_recv()
        at = part(g, axis, dest, lane)
        prod[at] = prod[at] + box(g, axis, rnd, way)[...]

    def product(g):
        for t in range(g * PER, g * PER + PER):
            out = jnp.dot(s_rel[t, 0], f_col[0], preferred_element_type=F32)
            for u in range(1, TC):
                out += jnp.dot(s_rel[t, u], f_col[u], preferred_element_type=F32)
            prod[t] = out.reshape(NZ, NY, 8, 256)

    def step(g, k):
        axes = ("y", "z") if KINDS[g] == "A" else ("z", "y")
        first = size[axes[0]] // 2
        if k == 0:
            product(g)
            for way in range(2):
                copy_of(g, axes[0], 0, way).start()
            return
        for way in range(2):
            if k <= first:
                take(g, axes[0], k - 1, way)
                if k < first:
                    copy_of(g, axes[0], k, way).start()
            else:
                take(g, axes[1], k - first - 1, way)
                if k < STEPS - 1:
                    copy_of(g, axes[1], k - first, way).start()
        if k == first:
            for way in range(2):
                copy_of(g, axes[1], 0, way).start()

    def slope_unit(n, acc):
        t, u = n // TC, n % TC
        cross = lax.dot_general(
            u_row[t // 4, t % 4], u_col[u], (((1,), (1,)), ((), ())), preferred_element_type=F32
        )
        across = norm_col[u]
        for k in range(0, 256, 32):
            down = norm_row[t, k : k + 32]
            norms = jnp.concatenate([down, down], axis=1) + across[0:1]
            minus = cross[k : k + 32] * (4.0 * LOG2E / 256.0) - norms
            term = s_rel[t, u, k : k + 32].astype(F32) * (minus * jnp.exp2(minus))
            acc = acc + jnp.sum(term.reshape(4, 8, 256), axis=0)
        return acc

    def ucol_forward():
        return pltpu.make_async_remote_copy(
            src_ref=u_col, dst_ref=u_col,
            send_sem=ucol_send.at[0], recv_sem=ucol_recv,
            device_id=sibling, device_id_type=MESH,
        )

    step(0, 0)
    step(1, 0)
    pltpu.make_async_copy(u_col, u_col, ucol_recv).wait()

    @pl.when(core == root % 2)
    def _():
        ucol_forward().start()

    step(2, 0)
    step(3, 0)
    for u in range(TC):
        cols = u_col[u].astype(F32)
        norm = lax.dot_general(
            jnp.ones((8, 256), F32), cols * cols, (((1,), (1,)), ((), ())),
            precision=HIGHEST, preferred_element_type=F32,
        )
        norm_col[u] = norm * (2.0 * LOG2E / 256.0)

    n_groups = len(KINDS)
    ticks = n_groups + STEPS - 1
    n_units = TR * TC
    busy = ticks - 2
    acc = jnp.zeros((8, 256), F32)
    done = 0
    for tick in range(1, ticks):
        for g in range(n_groups):
            k = tick - g
            if g < 4 and k <= 0:
                continue
            if 0 <= k < STEPS:
                step(g, k)
        until = min(n_units, (n_units * tick + busy - 1) // busy)
        if until > done:
            acc = lax.fori_loop(done, until, slope_unit, acc)
            done = until
    trail = jnp.sum(acc) * (-2.0 / LOG2E / 32768.0)

    for t in range(TR):
        total[pl.ds(t * 8, 8), :] = (
            c_ref[pl.ds((t // 2) * 16, 16), :].astype(F32)[(t % 2) * 8 : (t % 2) * 8 + 8]
            - 2.0 * prod[t, z, y]
        )
    whole = total[...]
    adjoint = jnp.dot(whole, b_ref[...], precision=HIGHEST, preferred_element_type=F32)
    adj_ref[...] = adjoint
    moment = lax.dot_general(
        whole, f_own[...].astype(F32), (((0,), (0,)), ((), ())),
        precision=HIGHEST, preferred_element_type=F32,
    )
    m1[:, 0:32, :] = moment.reshape(NR, 32, 256)

    panel = pd_ref[...].astype(F32)
    panel_norm = lax.dot_general(
        jnp.ones((8, 256), F32), panel * panel, (((1,), (1,)), ((), ())),
        precision=HIGHEST, preferred_element_type=F32,
    )
    first_row = pl.multiple_of((c // 2) * 16, 16)
    own = []
    for t in range(TR):
        pair = u_row[t // 4, t % 4, pl.ds(first_row, 16), :].astype(F32)
        own.append(jnp.where(c % 2 == 0, pair[0:8], pair[8:16]))
    own = jnp.concatenate(own, axis=0)
    own_norm = jnp.sum(own * own, axis=-1, keepdims=True)
    cross = lax.dot_general(
        own.astype(BF16), pd_ref[...], (((1,), (1,)), ((), ())), preferred_element_type=F32
    )
    scaled = (2.0 / 256.0) * (own_norm + panel_norm[0:1] - 2.0 * cross)
    panel_part = jnp.sum(adjoint * (2.0 * scaled * jnp.exp(-scaled))) * (1.0 / math.sqrt(8388608))
    lane = lax.broadcasted_iota(jnp.int32, (8, 256), 1)
    scalars = jnp.where(lane < 128, trail, panel_part)
    for j in range(NR):
        m1[j, 32:40, :] = scalars

    def exchange(stage, n, me, dev, src, dst):
        base = (0, 8, 12, 20, 24)[stage]

        def copy(d):
            peer = (me + d) % n
            return pltpu.make_async_remote_copy(
                src_ref=src(peer), dst_ref=dst.at[me],
                send_sem=m_send.at[base + d], recv_sem=m_recv.at[base + d],
                device_id=dev(peer), device_id_type=MESH,
            )

        @pl.loop(1, n)
        def _(d):
            copy(d).start()

        @pl.loop(1, n)
        def _(d):
            copy(d).wait()

    row_dev = lambda p: (p, c)
    y_dev = lambda p: (r, z * NY + p)
    z_dev = lambda p: (r, p * NY + y)

    m1r[r] = m1[r]
    exchange(0, NR, r, row_dev, lambda p: m1.at[p], m1r)
    part1 = m1r[0]
    for j in range(1, NR):
        part1 = part1 + m1r[j]
    for j in range(NY):
        m2[j, 0:8] = part1[8 * j : 8 * j + 8]
        m2[j, 8:16] = part1[32:40]
    m2r[y] = m2[y]
    exchange(1, NY, y, y_dev, lambda p: m2.at[p], m2r)
    m3[z] = ((m2r[0] + m2r[1]) + m2r[2]) + m2r[3]
    exchange(2, NZ, z, z_dev, lambda p: m3.at[z], m3)
    part3 = m3[0]
    for j in range(1, NZ):
        part3 = part3 + m3[j]
    m4[y] = part3[0:8]
    exchange(3, NY, y, y_dev, lambda p: m4.at[y], m4)
    m5[r] = m4[...].reshape(32, 256)
    exchange(4, NR, r, row_dev, lambda p: m5.at[r], m5)
    diag = lax.dot_general(
        b_ref[...], m5[...].reshape(256, 256), (((0,), (0,)), ((), ())),
        precision=HIGHEST, preferred_element_type=F32,
    )
    down = lax.broadcasted_iota(jnp.int32, (256, 256), 0)
    across = lax.broadcasted_iota(jnp.int32, (256, 256), 1)
    diag_ref[...] = jnp.where(down >= across, -diag, 0.0)
    slope_ref[...] = jnp.concatenate([part3[8:9, 0:1], part3[8:9, 128:129]], axis=1)

    @pl.loop(0, 16)
    def _(n):
        q, xd = n // NX, n % NX
        mine = jnp.logical_and(is_root, jnp.logical_and(q == quarter, xd == x))

        @pl.when(jnp.logical_not(mine))
        def _():
            pltpu.make_async_remote_copy(
                src_ref=f_hbm.at[q], dst_ref=f_buf.at[c % 2, c // 2],
                send_sem=f_send.at[n], recv_sem=f_recv.at[0],
                device_id=(2 * xd + c % 2, NR * q + r), device_id_type=MESH,
            ).wait_send()

    @pl.when(is_root)
    def _():
        for d in (1, 2, 3):
            ucol_to(d).wait_send()

    @pl.when(core == root % 2)
    def _():
        ucol_forward().wait_send()

    f_swap.wait_send()
    for g, kind in enumerate(KINDS):
        for axis in "yz":
            for rnd in range(size[axis] // 2):
                for way in range(2):
                    copy_of(g, axis, rnd, way).wait_send()


def local(trailing_cot, panel_factor, panel_cot, block_inverse, row_desc, panel_desc):
    s_rows = trailing_cot.reshape(TR, 256, TC, 2, 128).transpose(0, 1, 3, 2, 4).reshape(TR * 2048, 128)
    f_parts = panel_factor.reshape(4, 4, 8, 256).transpose(1, 0, 2, 3).reshape(4, 32, 256)
    hbm = pl.BlockSpec(memory_space=pl.ANY)
    vmem = pl.BlockSpec(memory_space=pltpu.VMEM)
    dma = pltpu.SemaphoreType.DMA
    V = pltpu.VMEM
    adjoint, diag, slope = pl.pallas_call(
        kernel,
        out_shape=(
            jax.ShapeDtypeStruct((128, 256), F32),
            jax.ShapeDtypeStruct((256, 256), F32),
            jax.ShapeDtypeStruct((1, 2), F32),
        ),
        in_specs=[hbm, hbm, hbm, vmem, vmem, vmem, vmem],
        out_specs=(vmem, vmem, vmem),
        scratch_shapes=[
            V((TR, 2048, 128), BF16),
            V((2048, 128), F32),
            V((TR, TC, 256, 256), BF16),
            V((4, 4, 256, 256), BF16),
            V((TC, 256, 256), BF16),
            V((TR, 256, 128), F32),
            V((TC, 8, 256), F32),
            V((2, 16, 32, 256), BF16),
            V((TC, 256, 256), BF16),
            V((TR, NZ, NY, 8, 256), F32),
            V((128, 256), F32),
            V((N_A, 2, PER, NZ, 8, 128), F32),
            V((N_A, 2, 1, PER, NZ, 8, 256), F32),
            V((N_A, 2, PER, 8, 128), F32),
            V((N_A, 2, 3, PER, 8, 256), F32),
            V((N_B, 2, PER, NY, 8, 128), F32),
            V((N_B, 2, 3, PER, NY, 8, 256), F32),
            V((N_B, 2, PER, 8, 128), F32),
            V((N_B, 2, 1, PER, 8, 256), F32),
            V((NR, 40, 256), F32),
            V((NR, 40, 256), F32),
            V((NY, 16, 256), F32),
            V((NY, 16, 256), F32),
            V((NZ, 16, 256), F32),
            V((NY, 8, 256), F32),
            V((NR, 32, 256), F32),
            dma((TR,)),
            dma,
            dma((16,)),
            dma((2,)),
            dma,
            dma((4,)),
            dma,
            dma((len(KINDS) * 12,)),
            dma((len(KINDS) * 12,)),
            dma((32,)),
            dma((32,)),
        ],
        compiler_params=pltpu.CompilerParams(
            collective_id=0, has_side_effects=True, vmem_limit_bytes=60 * 1024 * 1024
        ),
        cost_estimate=pl.CostEstimate(
            flops=4 * 4096 * 1024 * 256, bytes_accessed=12 * 1024 * 1024, transcendentals=4096 * 1024
        ),
        name="panel_step",
    )(
        f_parts,
        row_desc.reshape(4, 4, 256, 256),
        s_rows,
        panel_cot.reshape(128, 256),
        panel_factor.reshape(128, 256),
        block_inverse,
        panel_desc,
    )
    return adjoint.reshape(16, 8, 256), diag, slope.reshape(2)


def solution(mesh):
    in_specs = (
        P(None, "row", None, "col"),
        P(None, ("row", "col"), None),
        P(None, ("row", "col"), None),
        P(),
        P(None, "row", None),
        P(),
    )
    out_specs = (P(None, ("row", "col"), None), P(), P())
    return jax.shard_map(local, mesh=mesh, in_specs=in_specs, out_specs=out_specs, check_vma=False)
```

```python
import functools
import math

import jax
import jax.numpy as jnp
from jax import lax
from jax.experimental import pallas as pl
from jax.experimental.pallas import tpu as pltpu
from jax.sharding import PartitionSpec as P

MESH = pl.DeviceIdType.MESH
HIGHEST = lax.Precision.HIGHEST
F32 = jnp.float32
BF16 = jnp.bfloat16
LOG2E = math.log2(math.e)

TR = 16
TC = 4
NX, NY, NZ, NR = 4, 4, 8, 8
PER = 2
KINDS = "ABABABAA"
N_A = KINDS.count("A")
N_B = KINDS.count("B")
STEPS = 7


def kernel(
    u_hbm, s_hbm, c_ref, f_own, b_ref, pd_ref,
    adj_ref, diag_ref, slope_ref,
    s_raw, s_f32, s_rel, u_row, u_col, norm_row, norm_col, f_parts, f_buf, f_col, prod, total, near,
    ay1, ay2, az1, az2, bz1, bz2, by1, by2,
    m1, m1r, m3, m5,
    s_sem, u_sem, f_send, f_recv, f_local, ucol_send, ucol_recv, rs_send, rs_recv, m_send, m_recv,
):
    r = lax.axis_index("row")
    c = lax.axis_index("col")
    x, core = r // 2, r % 2
    z, y = c // NY, c % NY
    root = c % NR
    quarter = c // NR
    is_root = root == r
    feeds = core == y % 2
    place = r * NY + y

    def near_dev(p):
        return (p // NY, z * NY + p % NY)

    def partner(u):
        side = z + 1 - 2 * (z % 2) if u // 2 else z
        return side * NY + (y + 2 * (u % 2)) % NY

    barrier = pltpu.get_barrier_semaphore()

    def greet(dev):
        pl.semaphore_signal(barrier, inc=1, device_id=dev, device_id_type=MESH)

    @pl.loop(0, 16)
    def _(m):
        @pl.when(jnp.logical_not(jnp.logical_and(is_root, 2 * m + core == c)))
        def _():
            greet((root, 2 * m + core))

    @pl.loop(1, NR * NY)
    def _(d):
        greet(near_dev((place + d) % (NR * NY)))

    @pl.loop(1, NZ)
    def _(d):
        greet((r, ((z + d) % NZ) * NY + y))

    @pl.when(jnp.logical_and(feeds, jnp.logical_not(is_root)))
    def _():
        for u in range(TC):
            greet((root, partner(u)))

    s_copies = [
        pltpu.make_async_copy(s_hbm.at[pl.ds(t * 2048, 2048)], s_raw.at[t], s_sem.at[t])
        for t in range(TR)
    ]
    u_copy = pltpu.make_async_copy(u_hbm, u_row, u_sem)
    for cp in s_copies[:2]:
        cp.start()
    u_copy.start()
    for cp in s_copies[2:]:
        cp.start()

    f_wide = f_own[...].astype(F32)
    for q in range(4):
        f_parts[q] = jnp.concatenate(
            [f_wide[(4 * u + q) * 8 : (4 * u + q) * 8 + 8] for u in range(TC)], axis=0
        ).astype(BF16)

    pl.semaphore_wait(barrier, 16 + 31 + 7 - jnp.where(is_root, 1, 0) + jnp.where(feeds, 3, 0))

    @pl.loop(0, 16)
    def _(n):
        q, xd = n // NX, n % NX
        mine = jnp.logical_and(is_root, jnp.logical_and(q == quarter, xd == x))

        @pl.when(mine)
        def _():
            pltpu.make_async_copy(f_parts.at[q], f_buf.at[c % 2, c // 2], f_recv.at[0]).start()

        @pl.when(jnp.logical_not(mine))
        def _():
            pltpu.make_async_remote_copy(
                src_ref=f_parts.at[q], dst_ref=f_buf.at[c % 2, c // 2],
                send_sem=f_send.at[n], recv_sem=f_recv.at[0],
                device_id=(2 * xd + c % 2, NR * q + r), device_id_type=MESH,
            ).start()

    def ucol_to(u, d):
        return pltpu.make_async_remote_copy(
            src_ref=u_hbm.at[u, quarter], dst_ref=u_col.at[u],
            send_sem=ucol_send.at[d], recv_sem=ucol_recv,
            device_id=(((x + d) % NX) * 2 + core, partner(u)), device_id_type=MESH,
        )

    for u in range(TC):
        @pl.when(partner(u) % NR == r)
        def _():
            for d in (2, 1, 3):
                ucol_to(u, d).start()

    @pl.when(is_root)
    def _():
        pltpu.make_async_copy(u_hbm.at[:, quarter], u_col, ucol_recv).start()

    def relay(t):
        s_f32[...] = s_raw[t].astype(F32)
        for u in range(TC):
            for half in range(2):
                s_rel[t, u, :, half * 128 : half * 128 + 128] = s_f32[
                    pl.ds(half * 4 + u, 256, stride=8), :
                ].astype(BF16)

    for t in range(TR):
        s_copies[t].wait()

    @pl.loop(0, TR)
    def _(t):
        relay(t)

    u_copy.wait()

    @pl.loop(0, TR)
    def _(t):
        rows = u_row[t // 4, t % 4].astype(F32)
        norm = jnp.sum(rows * rows, axis=-1, keepdims=True) * (2.0 * LOG2E / 256.0)
        norm_row[t] = jnp.broadcast_to(norm, (256, 128))

    sibling = (2 * x + 1 - core, c)

    def ucol_forward():
        return pltpu.make_async_remote_copy(
            src_ref=u_col, dst_ref=u_col,
            send_sem=ucol_send.at[0], recv_sem=ucol_recv,
            device_id=sibling, device_id_type=MESH,
        )

    pltpu.make_async_copy(u_col, u_col, ucol_recv).wait()

    @pl.when(feeds)
    def _():
        ucol_forward().start()

    pltpu.make_async_copy(f_buf.at[0], f_buf.at[0], f_recv.at[0]).wait()
    f_swap = pltpu.make_async_remote_copy(
        src_ref=f_buf.at[core], dst_ref=f_buf.at[core],
        send_sem=f_local, recv_sem=f_recv.at[1],
        device_id=sibling, device_id_type=MESH,
    )
    f_swap.start()

    for u in range(TC):
        cols = u_col[u].astype(F32)
        norm = lax.dot_general(
            jnp.ones((8, 256), F32), cols * cols, (((1,), (1,)), ((), ())),
            precision=HIGHEST, preferred_element_type=F32,
        )
        norm_col[u] = norm * (2.0 * LOG2E / 256.0)

    panel = pd_ref[...].astype(F32)
    panel_norm = lax.dot_general(
        jnp.ones((8, 256), F32), panel * panel, (((1,), (1,)), ((), ())),
        precision=HIGHEST, preferred_element_type=F32,
    )
    first_row = pl.multiple_of((c // 2) * 16, 16)
    own = []
    for t in range(TR):
        pair = u_row[t // 4, t % 4, pl.ds(first_row, 16), :].astype(F32)
        own.append(jnp.where(c % 2 == 0, pair[0:8], pair[8:16]))
    own = jnp.concatenate(own, axis=0)
    own_norm = jnp.sum(own * own, axis=-1, keepdims=True)
    cross = lax.dot_general(
        own.astype(BF16), pd_ref[...], (((1,), (1,)), ((), ())), preferred_element_type=F32
    )
    scaled = (2.0 / 256.0) * (own_norm + panel_norm[0:1] - 2.0 * cross)
    near[...] = 2.0 * scaled * jnp.exp(-scaled) * (1.0 / math.sqrt(8388608))

    f_swap.wait_recv()

    @pl.loop(0, 16)
    def _(m):
        even = f_buf[0, m].astype(F32)
        odd = f_buf[1, m].astype(F32)
        for u in range(TC):
            rows = jnp.concatenate([even[8 * u : 8 * u + 8], odd[8 * u : 8 * u + 8]], axis=0)
            f_col[u, pl.ds(pl.multiple_of(m * 16, 16), 16), :] = rows.astype(BF16)

    neighbours = {
        "y": ((r, z * NY + (y + 1) % NY), (r, z * NY + (y + NY - 1) % NY)),
        "z": ((r, ((z + 1) % NZ) * NY + y), (r, ((z + NZ - 1) % NZ) * NY + y)),
    }
    size = {"y": NY, "z": NZ}
    here = {"y": y, "z": z}
    lanes = (pl.ds(0, 128), pl.ds(128, 128))
    full = pl.ds(0, 256)
    group_slot = {}
    for g, kind in enumerate(KINDS):
        group_slot[g] = KINDS[:g].count(kind)

    def part(g, axis, dest, lane):
        rows = pl.ds(g * PER, PER)
        if KINDS[g] == "A":
            if axis == "y":
                return (rows, slice(None), dest, slice(None), lane)
            return (rows, dest, y, slice(None), lane)
        if axis == "z":
            return (rows, dest, slice(None), slice(None), lane)
        return (rows, z, dest, slice(None), lane)

    def box(g, axis, rnd, way):
        slot = group_slot[g]
        if KINDS[g] == "A":
            first, later = (ay1, ay2) if axis == "y" else (az1, az2)
        else:
            first, later = (bz1, bz2) if axis == "z" else (by1, by2)
        if rnd == 0:
            return first.at[slot, way]
        return later.at[slot, way, rnd - 1]

    def sem_of(g, axis, rnd, way):
        second = axis == ("z" if KINDS[g] == "A" else "y")
        offset = (size["y"] // 2 if KINDS[g] == "A" else size["z"] // 2) if second else 0
        return (g * 6 + offset + rnd) * 2 + way

    def copy_of(g, axis, rnd, way):
        n = size[axis]
        reach = n // 2 - rnd
        sign = 1 if way == 0 else n - 1
        dest = (here[axis] + sign * reach) % n
        lane = lanes[way] if rnd == 0 else full
        k = sem_of(g, axis, rnd, way)
        return pltpu.make_async_remote_copy(
            src_ref=prod.at[part(g, axis, dest, lane)],
            dst_ref=box(g, axis, rnd, way),
            send_sem=rs_send.at[k], recv_sem=rs_recv.at[k],
            device_id=neighbours[axis][way], device_id_type=MESH,
        )

    def take(g, axis, rnd, way):
        n = size[axis]
        reach = n // 2 - rnd - 1
        sign = 1 if way == 0 else n - 1
        dest = (here[axis] + sign * reach) % n
        lane = lanes[way] if rnd == 0 else full
        copy_of(g, axis, rnd, way).wait_recv()
        at = part(g, axis, dest, lane)
        prod[at] = prod[at] + box(g, axis, rnd, way)[...]

    def product(g):
        for t in range(g * PER, g * PER + PER):
            out = jnp.dot(s_rel[t, 0], f_col[0], preferred_element_type=F32)
            for u in range(1, TC):
                out += jnp.dot(s_rel[t, u], f_col[u], preferred_element_type=F32)
            prod[t] = out.reshape(NZ, NY, 8, 256)

    def step(g, k):
        axes = ("y", "z") if KINDS[g] == "A" else ("z", "y")
        first = size[axes[0]] // 2
        if k == 0:
            product(g)
            for way in range(2):
                copy_of(g, axes[0], 0, way).start()
            return
        for way in range(2):
            if k <= first:
                take(g, axes[0], k - 1, way)
                if k < first:
                    copy_of(g, axes[0], k, way).start()
            else:
                take(g, axes[1], k - first - 1, way)
                if k < STEPS - 1:
                    copy_of(g, axes[1], k - first, way).start()
        if k == first:
            for way in range(2):
                copy_of(g, axes[1], 0, way).start()

    def slope_unit(n, acc):
        t, u = n // TC, n % TC
        cross = lax.dot_general(
            u_row[t // 4, t % 4], u_col[u], (((1,), (1,)), ((), ())), preferred_element_type=F32
        )
        across = norm_col[u]
        for k in range(0, 256, 32):
            down = norm_row[t, k : k + 32]
            norms = jnp.concatenate([down, down], axis=1) + across[0:1]
            minus = cross[k : k + 32] * (4.0 * LOG2E / 256.0) - norms
            term = s_rel[t, u, k : k + 32].astype(F32) * (minus * jnp.exp2(minus))
            acc = acc + jnp.sum(term.reshape(4, 8, 256), axis=0)
        return acc

    n_groups = len(KINDS)
    n_units = TR * TC
    acc = jnp.zeros((8, 256), F32)
    done = 0
    for g in range(n_groups):
        step(g, 0)
    visits = (STEPS - 1) * n_groups
    busy = visits - 4
    for visit in range(visits):
        until = min(n_units, n_units * (visit + 1) // busy)
        if until > done:
            acc = lax.fori_loop(done, until, slope_unit, acc)
            done = until
        step(visit % n_groups, 1 + visit // n_groups)
    trail = jnp.sum(acc) * (-2.0 / LOG2E / 32768.0)

    for t in range(TR):
        total[pl.ds(t * 8, 8), :] = (
            c_ref[pl.ds((t // 2) * 16, 16), :].astype(F32)[(t % 2) * 8 : (t % 2) * 8 + 8]
            - 2.0 * prod[t, z, y]
        )
    whole = total[...]
    adjoint = jnp.dot(whole, b_ref[...], precision=HIGHEST, preferred_element_type=F32)
    adj_ref[...] = adjoint
    moment = lax.dot_general(
        whole, f_own[...].astype(F32), (((0,), (0,)), ((), ())),
        precision=HIGHEST, preferred_element_type=F32,
    )
    panel_part = jnp.sum(adjoint * near[...])
    lane = lax.broadcasted_iota(jnp.int32, (8, 256), 1)
    down = lax.broadcasted_iota(jnp.int32, (8, 256), 0)
    for p in range(NR * NY):
        block = jnp.where(jnp.logical_and(down == 0, lane == 254), trail, moment[8 * p : 8 * p + 8])
        m1[p] = jnp.where(jnp.logical_and(down == 0, lane == 255), panel_part, block)

    def exchange(base, n, me, dev, src, dst):
        def copy(d):
            peer = (me + d) % n
            return pltpu.make_async_remote_copy(
                src_ref=src(peer), dst_ref=dst.at[me],
                send_sem=m_send.at[base + d], recv_sem=m_recv.at[base + d],
                device_id=dev(peer), device_id_type=MESH,
            )

        @pl.loop(1, n)
        def _(d):
            copy(d).start()

        @pl.loop(1, n)
        def _(d):
            copy(d).wait()

    m1r[place] = m1[place]
    exchange(0, NR * NY, place, near_dev, lambda p: m1.at[p], m1r)
    part1 = m1r[0]
    for j in range(1, NR * NY):
        part1 = part1 + m1r[j]
    m3[z] = part1
    exchange(32, NZ, z, lambda p: (r, p * NY + y), lambda p: m3.at[z], m3)
    part3 = m3[0]
    for j in range(1, NZ):
        part3 = part3 + m3[j]
    m5[place] = part3
    exchange(40, NR * NY, place, near_dev, lambda p: m5.at[place], m5)
    diag = lax.dot_general(
        b_ref[...], m5[...].reshape(256, 256), (((0,), (0,)), ((), ())),
        precision=HIGHEST, preferred_element_type=F32,
    )
    down = lax.broadcasted_iota(jnp.int32, (256, 256), 0)
    across = lax.broadcasted_iota(jnp.int32, (256, 256), 1)
    diag_ref[...] = jnp.where(down >= across, -diag, 0.0)
    slope_ref[...] = part3[0:1, 254:256]

    @pl.loop(0, 16)
    def _(n):
        q, xd = n // NX, n % NX
        mine = jnp.logical_and(is_root, jnp.logical_and(q == quarter, xd == x))

        @pl.when(jnp.logical_not(mine))
        def _():
            pltpu.make_async_remote_copy(
                src_ref=f_parts.at[q], dst_ref=f_buf.at[c % 2, c // 2],
                send_sem=f_send.at[n], recv_sem=f_recv.at[0],
                device_id=(2 * xd + c % 2, NR * q + r), device_id_type=MESH,
            ).wait_send()

    @pl.when(feeds)
    def _():
        for d in (1, 2, 3):
            ucol_to(0, d).wait_send()
        ucol_forward().wait_send()

    f_swap.wait_send()
    for g, kind in enumerate(KINDS):
        for axis in "yz":
            for rnd in range(size[axis] // 2):
                for way in range(2):
                    copy_of(g, axis, rnd, way).wait_send()


def local(trailing_cot, panel_factor, panel_cot, block_inverse, row_desc, panel_desc):
    s_rows = trailing_cot.reshape(TR, 256, TC, 2, 128).transpose(0, 1, 3, 2, 4).reshape(TR * 2048, 128)
    hbm = pl.BlockSpec(memory_space=pl.ANY)
    vmem = pl.BlockSpec(memory_space=pltpu.VMEM)
    dma = pltpu.SemaphoreType.DMA
    V = pltpu.VMEM
    adjoint, diag, slope = pl.pallas_call(
        kernel,
        out_shape=(
            jax.ShapeDtypeStruct((128, 256), F32),
            jax.ShapeDtypeStruct((256, 256), F32),
            jax.ShapeDtypeStruct((1, 2), F32),
        ),
        in_specs=[hbm, hbm, vmem, vmem, vmem, vmem],
        out_specs=(vmem, vmem, vmem),
        scratch_shapes=[
            V((TR, 2048, 128), BF16),
            V((2048, 128), F32),
            V((TR, TC, 256, 256), BF16),
            V((4, 4, 256, 256), BF16),
            V((TC, 256, 256), BF16),
            V((TR, 256, 128), F32),
            V((TC, 8, 256), F32),
            V((4, 32, 256), BF16),
            V((2, 16, 32, 256), BF16),
            V((TC, 256, 256), BF16),
            V((TR, NZ, NY, 8, 256), F32),
            V((128, 256), F32),
            V((128, 256), F32),
            V((N_A, 2, PER, NZ, 8, 128), F32),
            V((N_A, 2, 1, PER, NZ, 8, 256), F32),
            V((N_A, 2, PER, 8, 128), F32),
            V((N_A, 2, 3, PER, 8, 256), F32),
            V((N_B, 2, PER, NY, 8, 128), F32),
            V((N_B, 2, 3, PER, NY, 8, 256), F32),
            V((N_B, 2, PER, 8, 128), F32),
            V((N_B, 2, 1, PER, 8, 256), F32),
            V((NR * NY, 8, 256), F32),
            V((NR * NY, 8, 256), F32),
            V((NZ, 8, 256), F32),
            V((NR * NY, 8, 256), F32),
            dma((TR,)),
            dma,
            dma((16,)),
            dma((2,)),
            dma,
            dma((4,)),
            dma,
            dma((len(KINDS) * 12,)),
            dma((len(KINDS) * 12,)),
            dma((72,)),
            dma((72,)),
        ],
        compiler_params=pltpu.CompilerParams(
            collective_id=0, has_side_effects=True, vmem_limit_bytes=60 * 1024 * 1024
        ),
        cost_estimate=pl.CostEstimate(
            flops=4 * 4096 * 1024 * 256, bytes_accessed=12 * 1024 * 1024, transcendentals=4096 * 1024
        ),
        name="panel_step",
    )(
        row_desc.reshape(4, 4, 256, 256),
        s_rows,
        panel_cot.reshape(128, 256),
        panel_factor.reshape(128, 256),
        block_inverse,
        panel_desc,
    )
    return adjoint.reshape(16, 8, 256), diag, slope.reshape(2)


def solution(mesh):
    in_specs = (
        P(None, "row", None, "col"),
        P(None, ("row", "col"), None),
        P(None, ("row", "col"), None),
        P(),
        P(None, "row", None),
        P(),
    )
    out_specs = (P(None, ("row", "col"), None), P(), P())
    return jax.shard_map(local, mesh=mesh, in_specs=in_specs, out_specs=out_specs, check_vma=False)
```

```python
import functools
import math

import jax
import jax.numpy as jnp
from jax import lax
from jax.experimental import pallas as pl
from jax.experimental.pallas import tpu as pltpu
from jax.sharding import PartitionSpec as P

MESH = pl.DeviceIdType.MESH
HIGHEST = lax.Precision.HIGHEST
F32 = jnp.float32
BF16 = jnp.bfloat16
LOG2E = math.log2(math.e)

TR = 16
TC = 4
NX, NY, NZ, NR = 4, 4, 8, 8
PER = 2
KINDS = "ABABABAB"
N_A = KINDS.count("A")
N_B = KINDS.count("B")
EARLY = 6
STEPS = 7


def kernel(
    u_hbm, s_hbm, c_ref, f_own, b_ref, pd_ref,
    adj_ref, moment_ref, slope_ref,
    s_raw, s_f32, s_rel, u_row, u_col, norm_row, norm_col, f_parts, f_buf, f_col, f_z, f_y, prod, total, near_a, near_b, mt, pan,
    ay1, ay2, az1, az2, bz1, bz2, by1, by2,
    m1, m1r, m3, m5,
    s_sem, u_sem, f_send, f_recv, f_local, fz_send, fz_recv, ucol_send, ucol_recv, rs_send, rs_recv, m_send, m_recv,
):
    r = lax.axis_index("row")
    c = lax.axis_index("col")
    x, core = r // 2, r % 2
    z, y = c // NY, c % NY
    root = c % NR
    quarter = c // NR
    is_root = root == r
    feeds = core == y % 2
    place = r * NY + y

    def near_dev(p):
        return (p // NY, z * NY + p % NY)

    def partner(u):
        side = z + 1 - 2 * (z % 2) if u // 2 else z
        return side * NY + (y + 2 * (u % 2)) % NY

    barrier = pltpu.get_barrier_semaphore()

    def greet(dev):
        pl.semaphore_signal(barrier, inc=1, device_id=dev, device_id_type=MESH)

    @pl.loop(0, 16)
    def _(m):
        @pl.when(jnp.logical_not(jnp.logical_and(is_root, 2 * m + core == c)))
        def _():
            greet((root, 2 * m + core))

    @pl.loop(1, NR * NY)
    def _(d):
        greet(near_dev((place + d) % (NR * NY)))

    @pl.loop(1, NZ)
    def _(d):
        greet((r, ((z + d) % NZ) * NY + y))

    @pl.when(jnp.logical_and(feeds, jnp.logical_not(is_root)))
    def _():
        for u in range(TC):
            greet((root, partner(u)))

    s_copies = [
        pltpu.make_async_copy(s_hbm.at[pl.ds(t * 2048, 2048)], s_raw.at[t], s_sem.at[t])
        for t in range(TR)
    ]
    u_copy = pltpu.make_async_copy(u_hbm, u_row, u_sem)
    for cp in s_copies[:2]:
        cp.start()
    u_copy.start()
    for cp in s_copies[2:]:
        cp.start()

    f_wide = f_own[...].astype(F32)
    for q in range(4):
        f_parts[q] = jnp.concatenate(
            [f_wide[(4 * u + q) * 8 : (4 * u + q) * 8 + 8] for u in range(TC)], axis=0
        ).astype(BF16)

    for kind, store in (("A", f_z.at[z]), ("B", f_y.at[y])):
        for slot, g in enumerate(n for n, k in enumerate(KINDS) if k == kind):
            store[slot * 16 : slot * 16 + 16, :] = f_own[g * 16 : g * 16 + 16, :]

    def relay(t):
        s_f32[...] = s_raw[t].astype(F32)
        for u in range(TC):
            for half in range(2):
                s_rel[t, u, :, half * 128 : half * 128 + 128] = s_f32[
                    pl.ds(half * 4 + u, 256, stride=8), :
                ].astype(BF16)

    for t in range(EARLY):
        s_copies[t].wait()

    @pl.loop(0, EARLY)
    def _(t):
        relay(t)

    pl.semaphore_wait(barrier, 16 + 31 + 7 - jnp.where(is_root, 1, 0) + jnp.where(feeds, 3, 0))

    @pl.loop(0, 16)
    def _(n):
        q, xd = n // NX, n % NX
        mine = jnp.logical_and(is_root, jnp.logical_and(q == quarter, xd == x))

        @pl.when(mine)
        def _():
            pltpu.make_async_copy(f_parts.at[q], f_buf.at[c % 2, c // 2], f_recv.at[0]).start()

        @pl.when(jnp.logical_not(mine))
        def _():
            pltpu.make_async_remote_copy(
                src_ref=f_parts.at[q], dst_ref=f_buf.at[c % 2, c // 2],
                send_sem=f_send.at[n], recv_sem=f_recv.at[0],
                device_id=(2 * xd + c % 2, NR * q + r), device_id_type=MESH,
            ).start()

    def ucol_to(u, d):
        return pltpu.make_async_remote_copy(
            src_ref=u_hbm.at[u, quarter], dst_ref=u_col.at[u],
            send_sem=ucol_send.at[d], recv_sem=ucol_recv,
            device_id=(((x + d) % NX) * 2 + core, partner(u)), device_id_type=MESH,
        )

    for u in range(TC):
        @pl.when(partner(u) % NR == r)
        def _():
            for d in (2, 1, 3):
                ucol_to(u, d).start()

    @pl.when(is_root)
    def _():
        pltpu.make_async_copy(u_hbm.at[:, quarter], u_col, ucol_recv).start()

    def fz_to(d):
        return pltpu.make_async_remote_copy(
            src_ref=f_z.at[z], dst_ref=f_z.at[z],
            send_sem=fz_send.at[d], recv_sem=fz_recv.at[d],
            device_id=(r, ((z + d) % NZ) * NY + y), device_id_type=MESH,
        )

    def fy_to(d):
        return pltpu.make_async_remote_copy(
            src_ref=f_y.at[y], dst_ref=f_y.at[y],
            send_sem=fz_send.at[NZ + d], recv_sem=fz_recv.at[NZ + d],
            device_id=(r, z * NY + (y + d) % NY), device_id_type=MESH,
        )

    @pl.loop(1, NZ)
    def _(d):
        fz_to(d).start()

    @pl.loop(1, NY)
    def _(d):
        fy_to(d).start()

    for t in range(EARLY, TR):
        s_copies[t].wait()

    @pl.loop(EARLY, TR)
    def _(t):
        relay(t)

    u_copy.wait()

    @pl.loop(0, TR)
    def _(t):
        rows = u_row[t // 4, t % 4].astype(F32)
        norm = jnp.sum(rows * rows, axis=-1, keepdims=True) * (2.0 * LOG2E / 256.0)
        norm_row[t] = jnp.broadcast_to(norm, (256, 128))

    panel = pd_ref[...].astype(F32)
    panel_norm = lax.dot_general(
        jnp.ones((8, 256), F32), panel * panel, (((1,), (1,)), ((), ())),
        precision=HIGHEST, preferred_element_type=F32,
    )

    def weights(rows):
        norm = jnp.sum(rows * rows, axis=-1, keepdims=True)
        cross = lax.dot_general(
            rows.astype(BF16), pd_ref[...], (((1,), (1,)), ((), ())), preferred_element_type=F32
        )
        scaled = (2.0 / 256.0) * (norm + panel_norm[0:1] - 2.0 * cross)
        weight = 2.0 * scaled * jnp.exp(-scaled) * (1.0 / math.sqrt(8388608))
        return lax.dot_general(
            weight, b_ref[...], (((1,), (1,)), ((), ())),
            precision=HIGHEST, preferred_element_type=F32,
        )

    group_slot = {}
    for g, kind in enumerate(KINDS):
        group_slot[g] = KINDS[:g].count(kind)
    pan[...] = jnp.zeros((8, 256), F32)
    for g, kind in enumerate(KINDS):
        slot = group_slot[g]
        rows = []
        if kind == "A":
            for zz in range(NZ):
                for t in range(g * PER, g * PER + PER):
                    first = pl.multiple_of(zz * 32 + (y // 2) * 16, 16)
                    pair = u_row[t // 4, t % 4, pl.ds(first, 16), :].astype(F32)
                    rows.append(jnp.where(y % 2 == 0, pair[0:8], pair[8:16]))
            near, mine = near_a, z
        else:
            wide = [
                u_row[t // 4, t % 4, pl.ds(pl.multiple_of(z * 32, 32), 32), :].astype(F32)
                for t in range(g * PER, g * PER + PER)
            ]
            for yy in range(NY):
                for w in wide:
                    rows.append(w[yy * 8 : yy * 8 + 8])
            near, mine = near_b, y
        near[slot] = weights(jnp.concatenate(rows, axis=0))
        own_c = c_ref[g * 16 : g * 16 + 16, :].astype(F32)
        own_w = near[slot, pl.ds(pl.multiple_of(mine * 16, 16), 16), :]
        pan[...] += jnp.sum((own_c * own_w).reshape(2, 8, 256), axis=0)
    mt[...] = lax.dot_general(
        f_own[...], c_ref[...], (((0,), (0,)), ((), ())), preferred_element_type=F32
    )

    sibling = (2 * x + 1 - core, c)

    pltpu.make_async_copy(f_buf.at[0], f_buf.at[0], f_recv.at[0]).wait()
    f_swap = pltpu.make_async_remote_copy(
        src_ref=f_buf.at[core], dst_ref=f_buf.at[core],
        send_sem=f_local, recv_sem=f_recv.at[1],
        device_id=sibling, device_id_type=MESH,
    )
    f_swap.start()
    f_swap.wait_recv()

    @pl.loop(0, 16)
    def _(m):
        even = f_buf[0, m].astype(F32)
        odd = f_buf[1, m].astype(F32)
        for u in range(TC):
            rows = jnp.concatenate([even[8 * u : 8 * u + 8], odd[8 * u : 8 * u + 8]], axis=0)
            f_col[u, pl.ds(pl.multiple_of(m * 16, 16), 16), :] = rows.astype(BF16)

    neighbours = {
        "y": ((r, z * NY + (y + 1) % NY), (r, z * NY + (y + NY - 1) % NY)),
        "z": ((r, ((z + 1) % NZ) * NY + y), (r, ((z + NZ - 1) % NZ) * NY + y)),
    }
    size = {"y": NY, "z": NZ}
    here = {"y": y, "z": z}
    lanes = (pl.ds(0, 128), pl.ds(128, 128))
    full = pl.ds(0, 256)
    def part(g, axis, dest, lane):
        rows = pl.ds(g * PER, PER)
        if KINDS[g] == "A":
            if axis == "y":
                return (rows, slice(None), dest, slice(None), lane)
            return (rows, dest, y, slice(None), lane)
        if axis == "z":
            return (rows, dest, slice(None), slice(None), lane)
        return (rows, z, dest, slice(None), lane)

    def box(g, axis, rnd, way):
        slot = group_slot[g]
        if KINDS[g] == "A":
            first, later = (ay1, ay2) if axis == "y" else (az1, az2)
        else:
            first, later = (bz1, bz2) if axis == "z" else (by1, by2)
        if rnd == 0:
            return first.at[slot, way]
        return later.at[slot, way, rnd - 1]

    def sem_of(g, axis, rnd, way):
        second = axis == ("z" if KINDS[g] == "A" else "y")
        offset = (size["y"] // 2 if KINDS[g] == "A" else size["z"] // 2) if second else 0
        return (g * 6 + offset + rnd) * 2 + way

    def copy_of(g, axis, rnd, way):
        n = size[axis]
        reach = n // 2 - rnd
        sign = 1 if way == 0 else n - 1
        dest = (here[axis] + sign * reach) % n
        lane = lanes[way] if rnd == 0 else full
        k = sem_of(g, axis, rnd, way)
        return pltpu.make_async_remote_copy(
            src_ref=prod.at[part(g, axis, dest, lane)],
            dst_ref=box(g, axis, rnd, way),
            send_sem=rs_send.at[k], recv_sem=rs_recv.at[k],
            device_id=neighbours[axis][way], device_id_type=MESH,
        )

    def take(g, axis, rnd, way):
        n = size[axis]
        reach = n // 2 - rnd - 1
        sign = 1 if way == 0 else n - 1
        dest = (here[axis] + sign * reach) % n
        lane = lanes[way] if rnd == 0 else full
        copy_of(g, axis, rnd, way).wait_recv()
        at = part(g, axis, dest, lane)
        prod[at] = prod[at] + box(g, axis, rnd, way)[...]

    def product(g):
        for t in range(g * PER, g * PER + PER):
            out = jnp.dot(s_rel[t, 0], f_col[0], preferred_element_type=F32)
            for u in range(1, TC):
                out += jnp.dot(s_rel[t, u], f_col[u], preferred_element_type=F32)
            prod[t] = out.reshape(NZ, NY, 8, 256)

    def gather_moment(g):
        slot = group_slot[g]
        if KINDS[g] == "A":
            pieces = [prod[t, zz, y] for zz in range(NZ) for t in range(g * PER, g * PER + PER)]
            factor = f_z[:, slot * 16 : slot * 16 + 16, :].reshape(NZ * 16, 256)
            weight = near_a[slot]
        else:
            pieces = [prod[t, z, yy] for yy in range(NY) for t in range(g * PER, g * PER + PER)]
            factor = f_y[:, slot * 16 : slot * 16 + 16, :].reshape(NY * 16, 256)
            weight = near_b[slot]
        rows = jnp.concatenate(pieces, axis=0) * (-2.0)
        pan[...] += jnp.sum((rows * weight).reshape(-1, 8, 256), axis=0)
        flipped = jnp.transpose(factor.astype(F32)).astype(BF16)
        high = rows.astype(BF16)
        rest = rows - high.astype(F32)
        middle = rest.astype(BF16)
        low = (rest - middle.astype(F32)).astype(BF16)
        out = jnp.dot(flipped, low, preferred_element_type=F32)
        out += jnp.dot(flipped, middle, preferred_element_type=F32)
        out += jnp.dot(flipped, high, preferred_element_type=F32)
        mt[...] += out

    def step(g, k):
        axes = ("y", "z") if KINDS[g] == "A" else ("z", "y")
        first = size[axes[0]] // 2
        if k == 0:
            product(g)
            for way in range(2):
                copy_of(g, axes[0], 0, way).start()
            return
        for way in range(2):
            if k <= first:
                take(g, axes[0], k - 1, way)
                if k < first:
                    copy_of(g, axes[0], k, way).start()
            else:
                take(g, axes[1], k - first - 1, way)
                if k < STEPS - 1:
                    copy_of(g, axes[1], k - first, way).start()
        if k == first:
            for way in range(2):
                copy_of(g, axes[1], 0, way).start()
            gather_moment(g)

    def slope_row(t, acc):
        for u in range(TC):
            cross = lax.dot_general(
                u_row[t // 4, t % 4], u_col[u], (((1,), (1,)), ((), ())), preferred_element_type=F32
            )
            across = norm_col[u]
            for k in range(0, 256, 32):
                down = norm_row[t, k : k + 32]
                norms = jnp.concatenate([down, down], axis=1) + across[0:1]
                minus = cross[k : k + 32] * (4.0 * LOG2E / 256.0) - norms
                term = s_rel[t, u, k : k + 32].astype(F32) * (minus * jnp.exp2(minus))
                acc = acc + jnp.sum(term.reshape(4, 8, 256), axis=0)
        return acc

    def ucol_forward():
        return pltpu.make_async_remote_copy(
            src_ref=u_col, dst_ref=u_col,
            send_sem=ucol_send.at[0], recv_sem=ucol_recv,
            device_id=sibling, device_id_type=MESH,
        )

    n_groups = len(KINDS)
    for g in range(n_groups):
        step(g, 0)

    pltpu.make_async_copy(u_col, u_col, ucol_recv).wait()

    @pl.when(feeds)
    def _():
        ucol_forward().start()

    for u in range(TC):
        cols = u_col[u].astype(F32)
        norm = lax.dot_general(
            jnp.ones((8, 256), F32), cols * cols, (((1,), (1,)), ((), ())),
            precision=HIGHEST, preferred_element_type=F32,
        )
        norm_col[u] = norm * (2.0 * LOG2E / 256.0)

    for d in range(1, NZ):
        fz_to(d).wait_recv()
    for d in range(1, NY):
        fy_to(d).wait_recv()

    acc = jnp.zeros((8, 256), F32)
    done = 0
    for k in range(1, 5):
        if k < 3:
            for half in range(2):
                acc = lax.fori_loop(done, done + 4, slope_row, acc)
                done += 4
                for g in range(half * n_groups // 2, (half + 1) * n_groups // 2):
                    step(g, k)
        else:
            for g in range(n_groups):
                step(g, k)
    trail = jnp.sum(acc) * (-2.0 / LOG2E / 32768.0)
    panel_part = jnp.sum(pan[...])
    lane = lax.broadcasted_iota(jnp.int32, (8, 256), 1)
    down = lax.broadcasted_iota(jnp.int32, (8, 256), 0)
    for p in range(NR * NY):
        block = jnp.where(jnp.logical_and(down == 7, lane == 0), trail, mt[8 * p : 8 * p + 8])
        m1[p] = jnp.where(jnp.logical_and(down == 7, lane == 1), panel_part, block)

    def exchange(base, n, me, dev, src, dst):
        def copy(d):
            peer = (me + d) % n
            return pltpu.make_async_remote_copy(
                src_ref=src(peer), dst_ref=dst.at[me],
                send_sem=m_send.at[base + d], recv_sem=m_recv.at[base + d],
                device_id=dev(peer), device_id_type=MESH,
            )

        def start():
            @pl.loop(1, n)
            def _(d):
                copy(d).start()

        def wait():
            @pl.loop(1, n)
            def _(d):
                copy(d).wait()

        return start, wait

    start, wait = exchange(0, NR * NY, place, near_dev, lambda p: m1.at[p], m1r)
    m1r[place] = m1[place]
    start()
    for g in range(n_groups):
        step(g, 5)
    wait()
    part1 = m1r[0]
    for j in range(1, NR * NY):
        part1 = part1 + m1r[j]
    m3[z] = part1
    start, wait = exchange(32, NZ, z, lambda p: (r, p * NY + y), lambda p: m3.at[z], m3)
    start()
    for g in range(n_groups):
        step(g, 6)

    for t in range(TR):
        total[pl.ds(t * 8, 8), :] = (
            c_ref[pl.ds((t // 2) * 16, 16), :].astype(F32)[(t % 2) * 8 : (t % 2) * 8 + 8]
            - 2.0 * prod[t, z, y]
        )
    adj_ref[...] = jnp.dot(total[...], b_ref[...], precision=HIGHEST, preferred_element_type=F32)

    wait()
    part3 = m3[0]
    for j in range(1, NZ):
        part3 = part3 + m3[j]
    m5[place] = part3
    start, wait = exchange(40, NR * NY, place, near_dev, lambda p: m5.at[place], m5)
    start()
    slope_ref[...] = part3[7:8, 0:2]
    wait()
    moment_ref[...] = m5[...]

    @pl.loop(0, 16)
    def _(n):
        q, xd = n // NX, n % NX
        mine = jnp.logical_and(is_root, jnp.logical_and(q == quarter, xd == x))

        @pl.when(jnp.logical_not(mine))
        def _():
            pltpu.make_async_remote_copy(
                src_ref=f_parts.at[q], dst_ref=f_buf.at[c % 2, c // 2],
                send_sem=f_send.at[n], recv_sem=f_recv.at[0],
                device_id=(2 * xd + c % 2, NR * q + r), device_id_type=MESH,
            ).wait_send()

    @pl.when(feeds)
    def _():
        for d in (1, 2, 3):
            ucol_to(0, d).wait_send()
        ucol_forward().wait_send()

    f_swap.wait_send()
    for d in range(1, NZ):
        fz_to(d).wait_send()
    for d in range(1, NY):
        fy_to(d).wait_send()
    for g, kind in enumerate(KINDS):
        for axis in "yz":
            for rnd in range(size[axis] // 2):
                for way in range(2):
                    copy_of(g, axis, rnd, way).wait_send()


def finish(adj_in, m_in, slope_in, b_ref, adj_ref, diag_ref, slope_ref):
    adj_ref[...] = adj_in[...]
    slope_ref[...] = slope_in[...]
    diag = lax.dot_general(
        b_ref[...], m_in[...], (((0,), (1,)), ((), ())),
        precision=HIGHEST, preferred_element_type=F32,
    )
    down = lax.broadcasted_iota(jnp.int32, (256, 256), 0)
    across = lax.broadcasted_iota(jnp.int32, (256, 256), 1)
    diag_ref[...] = jnp.where(down >= across, -diag, 0.0)


def local(trailing_cot, panel_factor, panel_cot, block_inverse, row_desc, panel_desc):
    s_rows = trailing_cot.reshape(TR, 256, TC, 2, 128).transpose(0, 1, 3, 2, 4).reshape(TR * 2048, 128)
    hbm = pl.BlockSpec(memory_space=pl.ANY)
    vmem = pl.BlockSpec(memory_space=pltpu.VMEM)
    dma = pltpu.SemaphoreType.DMA
    V = pltpu.VMEM
    adjoint, moment, slope = pl.pallas_call(
        kernel,
        out_shape=(
            jax.ShapeDtypeStruct((128, 256), F32),
            jax.ShapeDtypeStruct((NR * NY, 8, 256), F32),
            jax.ShapeDtypeStruct((1, 2), F32),
        ),
        in_specs=[hbm, hbm, vmem, vmem, vmem, vmem],
        out_specs=(vmem, vmem, vmem),
        scratch_shapes=[
            V((TR, 2048, 128), BF16),
            V((2048, 128), F32),
            V((TR, TC, 256, 256), BF16),
            V((4, 4, 256, 256), BF16),
            V((TC, 256, 256), BF16),
            V((TR, 256, 128), F32),
            V((TC, 8, 256), F32),
            V((4, 32, 256), BF16),
            V((2, 16, 32, 256), BF16),
            V((TC, 256, 256), BF16),
            V((NZ, N_A * 16, 256), BF16),
            V((NY, N_B * 16, 256), BF16),
            V((TR, NZ, NY, 8, 256), F32),
            V((128, 256), F32),
            V((N_A, NZ * 16, 256), F32),
            V((N_B, NY * 16, 256), F32),
            V((256, 256), F32),
            V((8, 256), F32),
            V((N_A, 2, PER, NZ, 8, 128), F32),
            V((N_A, 2, 1, PER, NZ, 8, 256), F32),
            V((N_A, 2, PER, 8, 128), F32),
            V((N_A, 2, 3, PER, 8, 256), F32),
            V((N_B, 2, PER, NY, 8, 128), F32),
            V((N_B, 2, 3, PER, NY, 8, 256), F32),
            V((N_B, 2, PER, 8, 128), F32),
            V((N_B, 2, 1, PER, 8, 256), F32),
            V((NR * NY, 8, 256), F32),
            V((NR * NY, 8, 256), F32),
            V((NZ, 8, 256), F32),
            V((NR * NY, 8, 256), F32),
            dma((TR,)),
            dma,
            dma((16,)),
            dma((2,)),
            dma,
            dma((NZ + NY,)),
            dma((NZ + NY,)),
            dma((4,)),
            dma,
            dma((len(KINDS) * 12,)),
            dma((len(KINDS) * 12,)),
            dma((72,)),
            dma((72,)),
        ],
        compiler_params=pltpu.CompilerParams(
            collective_id=0, has_side_effects=True, vmem_limit_bytes=60 * 1024 * 1024
        ),
        cost_estimate=pl.CostEstimate(
            flops=4 * 4096 * 1024 * 256, bytes_accessed=12 * 1024 * 1024, transcendentals=4096 * 1024
        ),
        name="panel_step",
    )(
        row_desc.reshape(4, 4, 256, 256),
        s_rows,
        panel_cot.reshape(128, 256),
        panel_factor.reshape(128, 256),
        block_inverse,
        panel_desc,
    )
    adjoint, diag, slope = pl.pallas_call(
        finish,
        out_shape=(
            jax.ShapeDtypeStruct((128, 256), F32),
            jax.ShapeDtypeStruct((256, 256), F32),
            jax.ShapeDtypeStruct((1, 2), F32),
        ),
        in_specs=[vmem] * 4,
        out_specs=(vmem, vmem, vmem),
        name="finish",
    )(adjoint, moment.reshape(256, 256), slope, block_inverse)
    return adjoint.reshape(16, 8, 256), diag, slope.reshape(2)


def solution(mesh):
    in_specs = (
        P(None, "row", None, "col"),
        P(None, ("row", "col"), None),
        P(None, ("row", "col"), None),
        P(),
        P(None, "row", None),
        P(),
    )
    out_specs = (P(None, ("row", "col"), None), P(), P())
    return jax.shard_map(local, mesh=mesh, in_specs=in_specs, out_specs=out_specs, check_vma=False)
```

```python
import functools
import math

import jax
import jax.numpy as jnp
from jax import lax
from jax.experimental import pallas as pl
from jax.experimental.pallas import tpu as pltpu
from jax.sharding import PartitionSpec as P

MESH = pl.DeviceIdType.MESH
HIGHEST = lax.Precision.HIGHEST
F32 = jnp.float32
BF16 = jnp.bfloat16
LOG2E = math.log2(math.e)

TR = 16
TC = 4
NX, NY, NZ, NR = 4, 4, 8, 8
PER = 2
KINDS = "ABABABAB"
N_A = KINDS.count("A")
N_B = KINDS.count("B")
EARLY = 6
STEPS = 7


SCHEDULE = [
    ("send",), ("step", 7, 0), ("step", 3, 0), ("step", 5, 0), ("step", 1, 0), ("step", 6, 0), ("step", 7, 1),
    ("step", 2, 0), ("step", 3, 1), ("pass", 1), ("step", 4, 0), ("step", 5, 1), ("step", 1, 1),
    ("step", 0, 0), ("ucol",), ("slope", 1), ("step", 6, 1), ("step", 7, 2), ("slope", 1), ("pass", 2),
    ("slope", 1), ("step", 2, 1), ("step", 3, 2), ("slope", 1), ("slope", 1), ("step", 4, 1), ("step", 5, 2),
    ("slope", 1), ("pass", 3), ("slope", 1), ("step", 0, 1), ("step", 1, 2), ("slope", 1), ("slope", 1),
    ("step", 7, 3), ("slope", 1), ("slope", 1), ("step", 6, 2), ("step", 3, 3), ("factors",), ("moment", 6),
    ("slope", 1), ("slope", 1), ("step", 5, 3), ("slope", 1), ("slope", 1), ("step", 2, 2), ("step", 1, 3),
    ("moment", 2), ("slope", 1), ("step", 7, 4), ("step", 6, 3), ("moment", 7), ("step", 4, 2), ("moment", 4),
    ("step", 3, 4), ("moment", 3), ("step", 5, 4), ("step", 2, 3), ("moment", 5), ("step", 0, 2),
    ("step", 7, 5), ("moment", 0), ("step", 1, 4), ("step", 6, 4), ("step", 4, 3), ("step", 3, 5),
    ("moment", 1), ("sum1",), ("step", 2, 4), ("step", 0, 3), ("step", 5, 5), ("step", 7, 6), ("step", 1, 5),
    ("step", 6, 5), ("step", 4, 4), ("step", 3, 6), ("step", 2, 5), ("step", 0, 4), ("sum2",), ("step", 5, 6),
    ("step", 1, 6), ("step", 6, 6), ("step", 4, 5), ("step", 2, 6), ("step", 0, 5), ("step", 4, 6),
    ("step", 0, 6),
]


def kernel(
    u_hbm, s_hbm, c_hbm, f_hbm, b_hbm, pd_hbm,
    adj_hbm, moment_ref, slope_ref,
    c_ref, f_own, b_ref, pd_ref, adj_ref,
    s_raw, s_f32, s_rel, u_row, u_col, norm_row, norm_col, f_parts, f_buf, f_col, f_z, f_y, prod, total, near_a, near_b, q_a, q_b, mt, pan,
    ay1, ay2, az1, az2, bz1, bz2, by1, by2,
    m1, m1r, m3, m5,
    s_sem, in_sem, u_sem, f_send, f_recv, f_local, fz_send, fz_recv, ucol_send, ucol_recv, rs_send, rs_recv, m_send, m_recv,
):
    r = lax.axis_index("row")
    c = lax.axis_index("col")
    x, core = r // 2, r % 2
    z, y = c // NY, c % NY
    root = c % NR
    quarter = c // NR
    is_root = root == r
    feeds = core == y % 2
    place = r * NY + y

    def near_dev(p):
        return (p // NY, z * NY + p % NY)

    def partner(u):
        side = z + 1 - 2 * (z % 2) if u // 2 else z
        return side * NY + (y + 2 * (u % 2)) % NY

    barrier = pltpu.get_barrier_semaphore()

    def greet(dev):
        pl.semaphore_signal(barrier, inc=1, device_id=dev, device_id_type=MESH)

    @pl.loop(0, 16)
    def _(m):
        @pl.when(jnp.logical_not(jnp.logical_and(is_root, 2 * m + core == c)))
        def _():
            greet((root, 2 * m + core))

    @pl.loop(1, NR * NY)
    def _(d):
        greet(near_dev((place + d) % (NR * NY)))

    @pl.loop(1, NZ)
    def _(d):
        greet((r, ((z + d) % NZ) * NY + y))

    @pl.when(jnp.logical_and(feeds, jnp.logical_not(is_root)))
    def _():
        for u in range(TC):
            greet((root, partner(u)))

    s_copies = [
        pltpu.make_async_copy(s_hbm.at[pl.ds(t * 2048, 2048)], s_raw.at[t], s_sem.at[t])
        for t in range(TR)
    ]
    u_copy = pltpu.make_async_copy(u_hbm, u_row, u_sem)
    f_copy = pltpu.make_async_copy(f_hbm, f_own, in_sem.at[0])
    small = [
        pltpu.make_async_copy(c_hbm, c_ref, in_sem.at[1]),
        pltpu.make_async_copy(b_hbm, b_ref, in_sem.at[2]),
        pltpu.make_async_copy(pd_hbm, pd_ref, in_sem.at[3]),
    ]
    f_copy.start()
    for cp in s_copies[:2]:
        cp.start()
    u_copy.start()
    for cp in small:
        cp.start()
    for cp in s_copies[2:]:
        cp.start()

    f_copy.wait()
    f_wide = f_own[...].astype(F32)
    for q in range(4):
        f_parts[q] = jnp.concatenate(
            [f_wide[(4 * u + q) * 8 : (4 * u + q) * 8 + 8] for u in range(TC)], axis=0
        ).astype(BF16)

    for kind, store in (("A", f_z.at[z]), ("B", f_y.at[y])):
        for slot, g in enumerate(n for n, k in enumerate(KINDS) if k == kind):
            store[slot * 16 : slot * 16 + 16, :] = f_own[g * 16 : g * 16 + 16, :]

    def relay(t):
        s_f32[...] = s_raw[t].astype(F32)
        for u in range(TC):
            for half in range(2):
                s_rel[t, u, :, half * 128 : half * 128 + 128] = s_f32[
                    pl.ds(half * 4 + u, 256, stride=8), :
                ].astype(BF16)

    for t in range(EARLY):
        s_copies[t].wait()

    @pl.loop(0, EARLY)
    def _(t):
        relay(t)

    pl.semaphore_wait(barrier, 16 + 31 + 7 - jnp.where(is_root, 1, 0) + jnp.where(feeds, 3, 0))

    @pl.loop(0, 16)
    def _(n):
        q, xd = n // NX, n % NX
        mine = jnp.logical_and(is_root, jnp.logical_and(q == quarter, xd == x))

        @pl.when(mine)
        def _():
            pltpu.make_async_copy(f_parts.at[q], f_buf.at[c % 2, c // 2], f_recv.at[0]).start()

        @pl.when(jnp.logical_not(mine))
        def _():
            pltpu.make_async_remote_copy(
                src_ref=f_parts.at[q], dst_ref=f_buf.at[c % 2, c // 2],
                send_sem=f_send.at[n], recv_sem=f_recv.at[0],
                device_id=(2 * xd + c % 2, NR * q + r), device_id_type=MESH,
            ).start()

    def ucol_to(u, d):
        return pltpu.make_async_remote_copy(
            src_ref=u_hbm.at[u, quarter], dst_ref=u_col.at[u],
            send_sem=ucol_send.at[d], recv_sem=ucol_recv,
            device_id=(((x + d) % NX) * 2 + core, partner(u)), device_id_type=MESH,
        )

    for u in range(TC):
        @pl.when(partner(u) % NR == r)
        def _():
            for d in (2, 1, 3):
                ucol_to(u, d).start()

    @pl.when(is_root)
    def _():
        pltpu.make_async_copy(u_hbm.at[:, quarter], u_col, ucol_recv).start()

    def fz_to(rnd, way):
        sign = 1 if way == 0 else NZ - 1
        held = (z + (NZ - sign) * rnd) % NZ
        return pltpu.make_async_remote_copy(
            src_ref=f_z.at[held], dst_ref=f_z.at[held],
            send_sem=fz_send.at[4 * way + rnd], recv_sem=fz_recv.at[4 * way + rnd],
            device_id=(r, ((z + sign) % NZ) * NY + y), device_id_type=MESH,
        )

    def fy_to(d):
        return pltpu.make_async_remote_copy(
            src_ref=f_y.at[y], dst_ref=f_y.at[y],
            send_sem=fz_send.at[NZ + d], recv_sem=fz_recv.at[NZ + d],
            device_id=(r, z * NY + (y + d) % NY), device_id_type=MESH,
        )

    for t in range(EARLY, TR):
        s_copies[t].wait()

    @pl.loop(EARLY, TR)
    def _(t):
        relay(t)

    u_copy.wait()
    for cp in small:
        cp.wait()

    @pl.loop(0, TR)
    def _(t):
        rows = u_row[t // 4, t % 4].astype(F32)
        norm = jnp.sum(rows * rows, axis=-1, keepdims=True) * (2.0 * LOG2E / 256.0)
        norm_row[t] = jnp.broadcast_to(norm, (256, 128))

    panel = pd_ref[...].astype(F32)
    panel_norm = lax.dot_general(
        jnp.ones((8, 256), F32), panel * panel, (((1,), (1,)), ((), ())),
        precision=HIGHEST, preferred_element_type=F32,
    )

    def weights(rows):
        norm = jnp.sum(rows * rows, axis=-1, keepdims=True)
        cross = lax.dot_general(
            rows.astype(BF16), pd_ref[...], (((1,), (1,)), ((), ())), preferred_element_type=F32
        )
        scaled = (2.0 / 256.0) * (norm + panel_norm[0:1] - 2.0 * cross)
        weight = 2.0 * scaled * jnp.exp(-scaled) * (1.0 / math.sqrt(8388608))
        return lax.dot_general(
            weight, b_ref[...], (((1,), (1,)), ((), ())),
            precision=HIGHEST, preferred_element_type=F32,
        )

    group_slot = {}
    for g, kind in enumerate(KINDS):
        group_slot[g] = KINDS[:g].count(kind)
    pan[...] = jnp.zeros((8, 256), F32)
    for g, kind in enumerate(KINDS):
        slot = group_slot[g]
        rows = []
        if kind == "A":
            for zz in range(NZ):
                for t in range(g * PER, g * PER + PER):
                    first = pl.multiple_of(zz * 32 + (y // 2) * 16, 16)
                    pair = u_row[t // 4, t % 4, pl.ds(first, 16), :].astype(F32)
                    rows.append(jnp.where(y % 2 == 0, pair[0:8], pair[8:16]))
            near, mine = near_a, z
        else:
            wide = [
                u_row[t // 4, t % 4, pl.ds(pl.multiple_of(z * 32, 32), 32), :].astype(F32)
                for t in range(g * PER, g * PER + PER)
            ]
            for yy in range(NY):
                for w in wide:
                    rows.append(w[yy * 8 : yy * 8 + 8])
            near, mine = near_b, y
        near[slot] = weights(jnp.concatenate(rows, axis=0))
        own_c = c_ref[g * 16 : g * 16 + 16, :].astype(F32)
        own_w = near[slot, pl.ds(pl.multiple_of(mine * 16, 16), 16), :]
        pan[...] += jnp.sum((own_c * own_w).reshape(2, 8, 256), axis=0)
    mt[...] = lax.dot_general(
        f_own[...], c_ref[...], (((0,), (0,)), ((), ())), preferred_element_type=F32
    )

    sibling = (2 * x + 1 - core, c)

    pltpu.make_async_copy(f_buf.at[0], f_buf.at[0], f_recv.at[0]).wait()
    f_swap = pltpu.make_async_remote_copy(
        src_ref=f_buf.at[core], dst_ref=f_buf.at[core],
        send_sem=f_local, recv_sem=f_recv.at[1],
        device_id=sibling, device_id_type=MESH,
    )
    f_swap.start()

    f_swap.wait_recv()

    @pl.loop(0, 16, unroll=4)
    def _(m):
        even = f_buf[0, m].astype(F32)
        odd = f_buf[1, m].astype(F32)
        for u in range(TC):
            rows = jnp.concatenate([even[8 * u : 8 * u + 8], odd[8 * u : 8 * u + 8]], axis=0)
            f_col[u, pl.ds(pl.multiple_of(m * 16, 16), 16), :] = rows.astype(BF16)

    neighbours = {
        "y": ((r, z * NY + (y + 1) % NY), (r, z * NY + (y + NY - 1) % NY)),
        "z": ((r, ((z + 1) % NZ) * NY + y), (r, ((z + NZ - 1) % NZ) * NY + y)),
    }
    size = {"y": NY, "z": NZ}
    here = {"y": y, "z": z}
    lanes = (pl.ds(0, 128), pl.ds(128, 128))
    full = pl.ds(0, 256)
    def part(g, axis, dest, lane):
        rows = pl.ds(g * PER, PER)
        if KINDS[g] == "A":
            if axis == "y":
                return (rows, slice(None), dest, slice(None), lane)
            return (rows, dest, y, slice(None), lane)
        if axis == "z":
            return (rows, dest, slice(None), slice(None), lane)
        return (rows, z, dest, slice(None), lane)

    def box(g, axis, rnd, way):
        slot = group_slot[g]
        if KINDS[g] == "A":
            first, later = (ay1, ay2) if axis == "y" else (az1, az2)
        else:
            first, later = (bz1, bz2) if axis == "z" else (by1, by2)
        if rnd == 0:
            return first.at[slot, way]
        return later.at[slot, way, rnd - 1]

    def sem_of(g, axis, rnd, way):
        second = axis == ("z" if KINDS[g] == "A" else "y")
        offset = (size["y"] // 2 if KINDS[g] == "A" else size["z"] // 2) if second else 0
        return (g * 6 + offset + rnd) * 2 + way

    def copy_of(g, axis, rnd, way):
        n = size[axis]
        reach = n // 2 - rnd
        sign = 1 if way == 0 else n - 1
        dest = (here[axis] + sign * reach) % n
        lane = lanes[way] if rnd == 0 else full
        k = sem_of(g, axis, rnd, way)
        return pltpu.make_async_remote_copy(
            src_ref=prod.at[part(g, axis, dest, lane)],
            dst_ref=box(g, axis, rnd, way),
            send_sem=rs_send.at[k], recv_sem=rs_recv.at[k],
            device_id=neighbours[axis][way], device_id_type=MESH,
        )

    def take(g, axis, rnd, way):
        n = size[axis]
        reach = n // 2 - rnd - 1
        sign = 1 if way == 0 else n - 1
        dest = (here[axis] + sign * reach) % n
        lane = lanes[way] if rnd == 0 else full
        copy_of(g, axis, rnd, way).wait_recv()
        at = part(g, axis, dest, lane)
        prod[at] = prod[at] + box(g, axis, rnd, way)[...]

    def product(g):
        for t in range(g * PER, g * PER + PER):
            out = jnp.dot(s_rel[t, 0], f_col[0], preferred_element_type=F32)
            for u in range(1, TC):
                out += jnp.dot(s_rel[t, u], f_col[u], preferred_element_type=F32)
            prod[t] = out.reshape(NZ, NY, 8, 256)

    def keep_rows(g):
        slot = group_slot[g]
        span = range(g * PER, g * PER + PER)
        if KINDS[g] == "A":
            for n, piece in enumerate(prod[t, zz, y] for zz in range(NZ) for t in span):
                q_a[slot, n] = piece * (-2.0)
        else:
            for n, piece in enumerate(prod[t, z, yy] for yy in range(NY) for t in span):
                q_b[slot, n] = piece * (-2.0)

    def gather_moment(g):
        slot = group_slot[g]
        if KINDS[g] == "A":
            rows = q_a[slot].reshape(NZ * 16, 256)
            factor = f_z[:, slot * 16 : slot * 16 + 16, :].reshape(NZ * 16, 256)
            weight = near_a[slot]
        else:
            rows = q_b[slot].reshape(NY * 16, 256)
            factor = f_y[:, slot * 16 : slot * 16 + 16, :].reshape(NY * 16, 256)
            weight = near_b[slot]
        pan[...] += jnp.sum((rows * weight).reshape(-1, 8, 256), axis=0)
        flipped = jnp.transpose(factor.astype(F32)).astype(BF16)
        high = rows.astype(BF16)
        rest = rows - high.astype(F32)
        middle = rest.astype(BF16)
        low = (rest - middle.astype(F32)).astype(BF16)
        out = jnp.dot(flipped, low, preferred_element_type=F32)
        out += jnp.dot(flipped, middle, preferred_element_type=F32)
        out += jnp.dot(flipped, high, preferred_element_type=F32)
        mt[...] += out

    def step(g, k):
        axes = ("y", "z") if KINDS[g] == "A" else ("z", "y")
        first = size[axes[0]] // 2
        if k == 0:
            product(g)
            for way in range(2):
                copy_of(g, axes[0], 0, way).start()
            return
        for way in range(2):
            if k <= first:
                take(g, axes[0], k - 1, way)
                if k < first:
                    copy_of(g, axes[0], k, way).start()
            else:
                take(g, axes[1], k - first - 1, way)
                if k < STEPS - 1:
                    copy_of(g, axes[1], k - first, way).start()
        if k == first:
            for way in range(2):
                copy_of(g, axes[1], 0, way).start()
            keep_rows(g)

    def slope_row(t, acc):
        for u in range(TC):
            cross = lax.dot_general(
                u_row[t // 4, t % 4], u_col[u], (((1,), (1,)), ((), ())), preferred_element_type=F32
            )
            across = norm_col[u]
            for k in range(0, 256, 32):
                down = norm_row[t, k : k + 32]
                norms = jnp.concatenate([down, down], axis=1) + across[0:1]
                minus = cross[k : k + 32] * (4.0 * LOG2E / 256.0) - norms
                term = s_rel[t, u, k : k + 32].astype(F32) * (minus * jnp.exp2(minus))
                acc = acc + jnp.sum(term.reshape(4, 8, 256), axis=0)
        return acc

    def ucol_forward():
        return pltpu.make_async_remote_copy(
            src_ref=u_col, dst_ref=u_col,
            send_sem=ucol_send.at[0], recv_sem=ucol_recv,
            device_id=sibling, device_id_type=MESH,
        )

    n_groups = len(KINDS)

    def take_ucol():
        pltpu.make_async_copy(u_col, u_col, ucol_recv).wait()

        @pl.when(feeds)
        def _():
            ucol_forward().start()

        for u in range(TC):
            cols = u_col[u].astype(F32)
            norm = lax.dot_general(
                jnp.ones((8, 256), F32), cols * cols, (((1,), (1,)), ((), ())),
                precision=HIGHEST, preferred_element_type=F32,
            )
            norm_col[u] = norm * (2.0 * LOG2E / 256.0)

    def send_factors():
        for way in range(2):
            fz_to(0, way).start()

        @pl.loop(1, NY)
        def _(d):
            fy_to(d).start()

    def pass_factors(rnd):
        for way in range(2):
            fz_to(rnd - 1, way).wait_recv()
            if rnd + way < 4:
                fz_to(rnd, way).start()

    def take_factors():
        fz_to(3, 0).wait_recv()
        for d in range(1, NY):
            fy_to(d).wait_recv()

    near = []
    for dx in range(NX):
        for dk in range(2):
            for dy in range(NY):
                if dx or dk or dy:
                    near.append((min(dx, NX - dx) + min(dy, NY - dy) + 0.1 * dk, dx, dk, dy))
    near.sort(reverse=True)
    xs = [((x + d) % NX) * 2 for d in range(NX)]
    ks = [core, 1 - core]
    ys = [(y + d) % NY for d in range(NY)]

    def to_near(stage, src, dst):
        out = []
        for _, dx, dk, dy in near:
            row = xs[dx] + ks[dk]
            out.append(pltpu.make_async_remote_copy(
                src_ref=src(row * NY + ys[dy]), dst_ref=dst,
                send_sem=m_send.at[stage], recv_sem=m_recv.at[stage],
                device_id=(row, z * NY + ys[dy]), device_id_type=MESH,
            ))
        return out

    copies1 = to_near(0, lambda p: m1.at[p], m1r.at[place])
    copies3 = to_near(2, lambda p: m5.at[place], m5.at[place])
    copies2 = [
        pltpu.make_async_remote_copy(
            src_ref=m3.at[z], dst_ref=m3.at[z],
            send_sem=m_send.at[1], recv_sem=m_recv.at[1],
            device_id=(r, ((z + d) % NZ) * NY + y), device_id_type=MESH,
        )
        for d in (4, 3, 5, 2, 6, 1, 7)
    ]

    def wait_all(ref, n, sem):
        blocks = ref.at[pl.ds(0, n)]
        pltpu.make_async_copy(blocks, blocks, sem).wait()

    def sum_first(acc):
        trail = jnp.sum(acc) * (-2.0 / LOG2E / 32768.0)
        panel_part = jnp.sum(pan[...])
        lane = lax.broadcasted_iota(jnp.int32, (8, 256), 1)
        down = lax.broadcasted_iota(jnp.int32, (8, 256), 0)
        for p in range(NR * NY):
            block = jnp.where(jnp.logical_and(down == 7, lane == 0), trail, mt[8 * p : 8 * p + 8])
            m1[p] = jnp.where(jnp.logical_and(down == 7, lane == 1), panel_part, block)
        m1r[place] = m1[place]
        for cp in copies1:
            cp.start()

    def sum_second():
        wait_all(m1r, NR * NY - 1, m_recv.at[0])
        part = m1r[0]
        for j in range(1, NR * NY):
            part = part + m1r[j]
        m3[z] = part
        for cp in copies2:
            cp.start()

    def sum_third():
        wait_all(m3, NZ - 1, m_recv.at[1])
        part = m3[0]
        for j in range(1, NZ):
            part = part + m3[j]
        m5[place] = part
        for cp in copies3:
            cp.start()
        slope_ref[...] = part[7:8, 0:2]

    acc = jnp.zeros((8, 256), F32)
    done = 0
    for event in SCHEDULE:
        if event[0] == "step":
            step(event[1], event[2])
        elif event[0] == "slope":
            acc = lax.fori_loop(done, done + event[1], slope_row, acc)
            done += event[1]
        elif event[0] == "ucol":
            take_ucol()
        elif event[0] == "send":
            send_factors()
        elif event[0] == "pass":
            pass_factors(event[1])
        elif event[0] == "moment":
            gather_moment(event[1])
        elif event[0] == "factors":
            take_factors()
        elif event[0] == "sum1":
            sum_first(acc)
        elif event[0] == "sum2":
            sum_second()

    for t in range(TR):
        total[pl.ds(t * 8, 8), :] = (
            c_ref[pl.ds((t // 2) * 16, 16), :].astype(F32)[(t % 2) * 8 : (t % 2) * 8 + 8]
            - 2.0 * prod[t, z, y]
        )
    adj_ref[...] = jnp.dot(total[...], b_ref[...], precision=HIGHEST, preferred_element_type=F32)
    adj_copy = pltpu.make_async_copy(adj_ref, adj_hbm, in_sem.at[4])
    adj_copy.start()

    sum_third()
    wait_all(m5, NR * NY - 1, m_recv.at[2])
    moment_ref[...] = m5[...]

    adj_copy.wait()
    wait_all(m1r, NR * NY - 1, m_send.at[0])
    wait_all(m3, NZ - 1, m_send.at[1])
    wait_all(m5, NR * NY - 1, m_send.at[2])
    @pl.loop(0, 16)
    def _(n):
        q, xd = n // NX, n % NX
        mine = jnp.logical_and(is_root, jnp.logical_and(q == quarter, xd == x))

        @pl.when(jnp.logical_not(mine))
        def _():
            pltpu.make_async_remote_copy(
                src_ref=f_parts.at[q], dst_ref=f_buf.at[c % 2, c // 2],
                send_sem=f_send.at[n], recv_sem=f_recv.at[0],
                device_id=(2 * xd + c % 2, NR * q + r), device_id_type=MESH,
            ).wait_send()

    @pl.when(feeds)
    def _():
        for d in (1, 2, 3):
            ucol_to(0, d).wait_send()
        ucol_forward().wait_send()

    f_swap.wait_send()
    for rnd in range(4):
        for way in range(2):
            if rnd + way < 4:
                fz_to(rnd, way).wait_send()
    for d in range(1, NY):
        fy_to(d).wait_send()
    for g, kind in enumerate(KINDS):
        for axis in "yz":
            for rnd in range(size[axis] // 2):
                for way in range(2):
                    copy_of(g, axis, rnd, way).wait_send()


def finish(adj_in, m_in, slope_in, b_ref, adj_ref, diag_ref, slope_ref):
    adj_ref[...] = adj_in[...]
    slope_ref[...] = slope_in[...]
    diag = lax.dot_general(
        b_ref[...], m_in[...], (((0,), (1,)), ((), ())),
        precision=HIGHEST, preferred_element_type=F32,
    )
    down = lax.broadcasted_iota(jnp.int32, (256, 256), 0)
    across = lax.broadcasted_iota(jnp.int32, (256, 256), 1)
    diag_ref[...] = jnp.where(down >= across, -diag, 0.0)


def local(trailing_cot, panel_factor, panel_cot, block_inverse, row_desc, panel_desc):
    s_rows = trailing_cot.reshape(TR, 256, TC, 2, 128).transpose(0, 1, 3, 2, 4).reshape(TR * 2048, 128)
    hbm = pl.BlockSpec(memory_space=pl.ANY)
    vmem = pl.BlockSpec(memory_space=pltpu.VMEM)
    dma = pltpu.SemaphoreType.DMA
    V = pltpu.VMEM
    adjoint, moment, slope = pl.pallas_call(
        kernel,
        out_shape=(
            jax.ShapeDtypeStruct((128, 256), F32),
            jax.ShapeDtypeStruct((NR * NY, 8, 256), F32),
            jax.ShapeDtypeStruct((1, 2), F32),
        ),
        in_specs=[hbm] * 6,
        out_specs=(hbm, vmem, vmem),
        scratch_shapes=[
            V((128, 256), BF16),
            V((128, 256), BF16),
            V((256, 256), F32),
            V((256, 256), BF16),
            V((128, 256), F32),
            V((TR, 2048, 128), BF16),
            V((2048, 128), F32),
            V((TR, TC, 256, 256), BF16),
            V((4, 4, 256, 256), BF16),
            V((TC, 256, 256), BF16),
            V((TR, 256, 128), F32),
            V((TC, 8, 256), F32),
            V((4, 32, 256), BF16),
            V((2, 16, 32, 256), BF16),
            V((TC, 256, 256), BF16),
            V((NZ, N_A * 16, 256), BF16),
            V((NY, N_B * 16, 256), BF16),
            V((TR, NZ, NY, 8, 256), F32),
            V((128, 256), F32),
            V((N_A, NZ * 16, 256), F32),
            V((N_B, NY * 16, 256), F32),
            V((N_A, NZ * 2, 8, 256), F32),
            V((N_B, NY * 2, 8, 256), F32),
            V((256, 256), F32),
            V((8, 256), F32),
            V((N_A, 2, PER, NZ, 8, 128), F32),
            V((N_A, 2, 1, PER, NZ, 8, 256), F32),
            V((N_A, 2, PER, 8, 128), F32),
            V((N_A, 2, 3, PER, 8, 256), F32),
            V((N_B, 2, PER, NY, 8, 128), F32),
            V((N_B, 2, 3, PER, NY, 8, 256), F32),
            V((N_B, 2, PER, 8, 128), F32),
            V((N_B, 2, 1, PER, 8, 256), F32),
            V((NR * NY, 8, 256), F32),
            V((NR * NY, 8, 256), F32),
            V((NZ, 8, 256), F32),
            V((NR * NY, 8, 256), F32),
            dma((TR,)),
            dma((5,)),
            dma,
            dma((16,)),
            dma((2,)),
            dma,
            dma((NZ + NY,)),
            dma((NZ + NY,)),
            dma((4,)),
            dma,
            dma((len(KINDS) * 12,)),
            dma((len(KINDS) * 12,)),
            dma((3,)),
            dma((3,)),
        ],
        compiler_params=pltpu.CompilerParams(
            collective_id=0, has_side_effects=True, vmem_limit_bytes=60 * 1024 * 1024
        ),
        cost_estimate=pl.CostEstimate(
            flops=4 * 4096 * 1024 * 256, bytes_accessed=12 * 1024 * 1024, transcendentals=4096 * 1024
        ),
        name="panel_step",
    )(
        row_desc.reshape(4, 4, 256, 256),
        s_rows,
        panel_cot.reshape(128, 256),
        panel_factor.reshape(128, 256),
        block_inverse,
        panel_desc,
    )
    adjoint, diag, slope = pl.pallas_call(
        finish,
        out_shape=(
            jax.ShapeDtypeStruct((128, 256), F32),
            jax.ShapeDtypeStruct((256, 256), F32),
            jax.ShapeDtypeStruct((1, 2), F32),
        ),
        in_specs=[vmem] * 4,
        out_specs=(vmem, vmem, vmem),
        name="finish",
    )(adjoint, moment.reshape(256, 256), slope, block_inverse)
    return adjoint.reshape(16, 8, 256), diag, slope.reshape(2)


def solution(mesh):
    in_specs = (
        P(None, "row", None, "col"),
        P(None, ("row", "col"), None),
        P(None, ("row", "col"), None),
        P(),
        P(None, "row", None),
        P(),
    )
    out_specs = (P(None, ("row", "col"), None), P(), P())
    return jax.shard_map(local, mesh=mesh, in_specs=in_specs, out_specs=out_specs, check_vma=False)
```

```python
import functools
import math

import jax
import jax.numpy as jnp
from jax import lax
from jax.experimental import pallas as pl
from jax.experimental.pallas import tpu as pltpu
from jax.sharding import PartitionSpec as P

MESH = pl.DeviceIdType.MESH
HIGHEST = lax.Precision.HIGHEST
F32 = jnp.float32
BF16 = jnp.bfloat16
LOG2E = math.log2(math.e)

TR = 16
TC = 4
NX, NY, NZ, NR = 4, 4, 8, 8
PER = 2
KINDS = "ABABABAB"
N_A = KINDS.count("A")
N_B = KINDS.count("B")
EARLY = 3
STEPS = 7


SCHEDULE = [
    ("send",), ("step", 7, 0), ("step", 3, 0), ("step", 5, 0), ("step", 1, 0), ("step", 6, 0), ("step", 7, 1),
    ("step", 2, 0), ("step", 3, 1), ("pass", 1), ("step", 4, 0), ("upass",), ("step", 5, 1), ("step", 1, 1),
    ("step", 0, 0), ("ucol",), ("slope", 1), ("step", 6, 1), ("step", 7, 2), ("slope", 1), ("pass", 2),
    ("slope", 1), ("step", 2, 1), ("step", 3, 2), ("slope", 1), ("slope", 1), ("step", 4, 1), ("step", 5, 2),
    ("slope", 1), ("pass", 3), ("slope", 1), ("step", 0, 1), ("step", 1, 2), ("slope", 1), ("slope", 1),
    ("step", 7, 3), ("slope", 1), ("slope", 1), ("step", 6, 2), ("step", 3, 3), ("factors",), ("moment", 6),
    ("slope", 1), ("slope", 1), ("step", 5, 3), ("slope", 1), ("slope", 1), ("step", 2, 2), ("step", 1, 3),
    ("moment", 2), ("slope", 1), ("step", 7, 4), ("step", 6, 3), ("moment", 7), ("step", 4, 2), ("moment", 4),
    ("step", 3, 4), ("moment", 3), ("step", 5, 4), ("step", 2, 3), ("moment", 5), ("step", 0, 2),
    ("step", 7, 5), ("moment", 0), ("step", 1, 4), ("step", 6, 4), ("step", 4, 3), ("step", 3, 5),
    ("moment", 1), ("sum1",), ("step", 2, 4), ("step", 0, 3), ("step", 5, 5), ("step", 7, 6), ("step", 1, 5),
    ("step", 6, 5), ("step", 4, 4), ("step", 3, 6), ("step", 2, 5), ("step", 0, 4), ("sum2",), ("step", 5, 6),
    ("step", 1, 6), ("step", 6, 6), ("step", 4, 5), ("step", 2, 6), ("step", 0, 5), ("step", 4, 6),
    ("step", 0, 6),
]


def kernel(
    u_hbm, s_hbm, c_hbm, f_hbm, b_hbm, pd_hbm,
    adj_hbm, moment_ref, slope_ref,
    c_ref, f_own, b_ref, pd_ref, adj_ref,
    s_raw, s_f32, s_rel, u_row, u_col, norm_row, norm_col, f_parts, f_buf, f_col, f_z, f_y, prod, total, near_a, near_b, q_a, q_b, mt, pan,
    ay1, ay2, az1, az2, bz1, bz2, by1, by2,
    m1, m1r, m3, m5,
    s_sem, in_sem, u_sem, f_send, f_recv, f_local, fz_send, fz_recv, ucol_send, ucol_recv, rs_send, rs_recv, m_send, m_recv,
):
    r = lax.axis_index("row")
    c = lax.axis_index("col")
    x, core = r // 2, r % 2
    z, y = c // NY, c % NY
    root = c % NR
    quarter = c // NR
    is_root = root == r
    feeds = core == y % 2
    place = r * NY + y

    def near_dev(p):
        return (p // NY, z * NY + p % NY)

    def partner(u):
        side = z + 1 - 2 * (z % 2) if u // 2 else z
        return side * NY + (y + 2 * (u % 2)) % NY

    barrier = pltpu.get_barrier_semaphore()

    def greet(dev):
        pl.semaphore_signal(barrier, inc=1, device_id=dev, device_id_type=MESH)

    @pl.loop(0, 16)
    def _(m):
        @pl.when(jnp.logical_not(jnp.logical_and(is_root, 2 * m + core == c)))
        def _():
            greet((root, 2 * m + core))

    @pl.when(jnp.logical_and(feeds, jnp.logical_not(is_root)))
    def _():
        for u in range(TC):
            greet((root, partner(u)))

    xs = [((x + d) % NX) * 2 for d in range(NX)]
    ks = [core, 1 - core]
    ys = [(y + d) % NY for d in range(NY)]
    for dx in (2, 1, 3, 0):
        for dy in (2, 1, 3, 0):
            for dk in range(2):
                if dx or dk or dy:
                    greet((xs[dx] + ks[dk], z * NY + ys[dy]))

    @pl.loop(1, NZ)
    def _(d):
        greet((r, ((z + d) % NZ) * NY + y))

    s_copies = [
        pltpu.make_async_copy(s_hbm.at[pl.ds(t * 2048, 2048)], s_raw.at[t], s_sem.at[t])
        for t in range(TR)
    ]
    u_copy = pltpu.make_async_copy(u_hbm, u_row, u_sem)
    f_copy = pltpu.make_async_copy(f_hbm, f_own, in_sem.at[0])
    small = [
        pltpu.make_async_copy(c_hbm, c_ref, in_sem.at[1]),
        pltpu.make_async_copy(b_hbm, b_ref, in_sem.at[2]),
        pltpu.make_async_copy(pd_hbm, pd_ref, in_sem.at[3]),
    ]
    f_copy.start()
    for cp in s_copies[:2]:
        cp.start()
    u_copy.start()
    for cp in small:
        cp.start()
    for cp in s_copies[2:]:
        cp.start()

    f_copy.wait()
    f_wide = f_own[...].astype(F32)
    for q in range(4):
        f_parts[q] = jnp.concatenate(
            [f_wide[(4 * u + q) * 8 : (4 * u + q) * 8 + 8] for u in range(TC)], axis=0
        ).astype(BF16)

    for kind, store in (("A", f_z.at[z]), ("B", f_y.at[y])):
        for slot, g in enumerate(n for n, k in enumerate(KINDS) if k == kind):
            store[slot * 16 : slot * 16 + 16, :] = f_own[g * 16 : g * 16 + 16, :]

    def relay(t):
        s_f32[...] = s_raw[t].astype(F32)
        for u in range(TC):
            for half in range(2):
                s_rel[t, u, :, half * 128 : half * 128 + 128] = s_f32[
                    pl.ds(half * 4 + u, 256, stride=8), :
                ].astype(BF16)

    for t in range(EARLY):
        s_copies[t].wait()

    @pl.loop(0, EARLY)
    def _(t):
        relay(t)

    pl.semaphore_wait(barrier, 16 + 31 + 7 - jnp.where(is_root, 1, 0) + jnp.where(feeds, 3, 0))

    def far_first(n):
        dq, dx = n // NX, n % NX
        dq = jnp.where(dq < 2, 2 - dq, 3 * (3 - dq))
        dx = jnp.where(dx < 2, 2 - dx, 3 * (3 - dx))
        return (z // 2 + dq) % 4, (x + dx) % NX

    @pl.loop(0, 16)
    def _(n):
        q, xd = far_first(n)
        mine = jnp.logical_and(is_root, jnp.logical_and(q == quarter, xd == x))

        @pl.when(mine)
        def _():
            pltpu.make_async_copy(f_parts.at[q], f_buf.at[c % 2, c // 2], f_recv.at[0]).start()

        @pl.when(jnp.logical_not(mine))
        def _():
            pltpu.make_async_remote_copy(
                src_ref=f_parts.at[q], dst_ref=f_buf.at[c % 2, c // 2],
                send_sem=f_send.at[n], recv_sem=f_recv.at[0],
                device_id=(2 * xd + c % 2, NR * q + r), device_id_type=MESH,
            ).start()

    def ucol_to(u, d):
        return pltpu.make_async_remote_copy(
            src_ref=u_hbm.at[u, quarter], dst_ref=u_col.at[u],
            send_sem=ucol_send.at[d], recv_sem=ucol_recv,
            device_id=(((x + d) % NX) * 2 + core, partner(u)), device_id_type=MESH,
        )

    def send_ucol():
        for u in range(TC):
            @pl.when(partner(u) % NR == r)
            def _():
                for d in (2, 1, 3):
                    ucol_to(u, d).start()

        @pl.when(is_root)
        def _():
            pltpu.make_async_copy(u_hbm.at[:, quarter], u_col, ucol_recv).start()

    send_ucol()

    def fz_to(rnd, way):
        sign = 1 if way == 0 else NZ - 1
        held = (z + (NZ - sign) * rnd) % NZ
        return pltpu.make_async_remote_copy(
            src_ref=f_z.at[held], dst_ref=f_z.at[held],
            send_sem=fz_send.at[4 * way + rnd], recv_sem=fz_recv.at[4 * way + rnd],
            device_id=(r, ((z + sign) % NZ) * NY + y), device_id_type=MESH,
        )

    def fy_to(d):
        return pltpu.make_async_remote_copy(
            src_ref=f_y.at[y], dst_ref=f_y.at[y],
            send_sem=fz_send.at[NZ + d], recv_sem=fz_recv.at[NZ + d],
            device_id=(r, z * NY + (y + d) % NY), device_id_type=MESH,
        )

    for t in range(EARLY, TR):
        s_copies[t].wait()

    @pl.loop(EARLY, TR)
    def _(t):
        relay(t)

    u_copy.wait()
    for cp in small:
        cp.wait()

    @pl.loop(0, TR)
    def _(t):
        rows = u_row[t // 4, t % 4].astype(F32)
        norm = jnp.sum(rows * rows, axis=-1, keepdims=True) * (2.0 * LOG2E / 256.0)
        norm_row[t] = jnp.broadcast_to(norm, (256, 128))

    panel = pd_ref[...].astype(F32)
    panel_norm = lax.dot_general(
        jnp.ones((8, 256), F32), panel * panel, (((1,), (1,)), ((), ())),
        precision=HIGHEST, preferred_element_type=F32,
    )

    def weights(rows):
        norm = jnp.sum(rows * rows, axis=-1, keepdims=True)
        cross = lax.dot_general(
            rows.astype(BF16), pd_ref[...], (((1,), (1,)), ((), ())), preferred_element_type=F32
        )
        scaled = (2.0 / 256.0) * (norm + panel_norm[0:1] - 2.0 * cross)
        weight = 2.0 * scaled * jnp.exp(-scaled) * (1.0 / math.sqrt(8388608))
        return lax.dot_general(
            weight, b_ref[...], (((1,), (1,)), ((), ())),
            precision=HIGHEST, preferred_element_type=F32,
        )

    group_slot = {}
    for g, kind in enumerate(KINDS):
        group_slot[g] = KINDS[:g].count(kind)
    pan[...] = jnp.zeros((8, 256), F32)
    for g, kind in enumerate(KINDS):
        slot = group_slot[g]
        rows = []
        if kind == "A":
            for zz in range(NZ):
                for t in range(g * PER, g * PER + PER):
                    first = pl.multiple_of(zz * 32 + (y // 2) * 16, 16)
                    pair = u_row[t // 4, t % 4, pl.ds(first, 16), :].astype(F32)
                    rows.append(jnp.where(y % 2 == 0, pair[0:8], pair[8:16]))
            near, mine = near_a, z
        else:
            wide = [
                u_row[t // 4, t % 4, pl.ds(pl.multiple_of(z * 32, 32), 32), :].astype(F32)
                for t in range(g * PER, g * PER + PER)
            ]
            for yy in range(NY):
                for w in wide:
                    rows.append(w[yy * 8 : yy * 8 + 8])
            near, mine = near_b, y
        near[slot] = weights(jnp.concatenate(rows, axis=0))
        own_c = c_ref[g * 16 : g * 16 + 16, :].astype(F32)
        own_w = near[slot, pl.ds(pl.multiple_of(mine * 16, 16), 16), :]
        pan[...] += jnp.sum((own_c * own_w).reshape(2, 8, 256), axis=0)
    mt[...] = lax.dot_general(
        f_own[...], c_ref[...], (((0,), (0,)), ((), ())), preferred_element_type=F32
    )

    sibling = (2 * x + 1 - core, c)

    pltpu.make_async_copy(f_buf.at[0], f_buf.at[0], f_recv.at[0]).wait()
    f_swap = pltpu.make_async_remote_copy(
        src_ref=f_buf.at[core], dst_ref=f_buf.at[core],
        send_sem=f_local, recv_sem=f_recv.at[1],
        device_id=sibling, device_id_type=MESH,
    )
    f_swap.start()

    f_swap.wait_recv()

    @pl.loop(0, 16, unroll=4)
    def _(m):
        even = f_buf[0, m].astype(F32)
        odd = f_buf[1, m].astype(F32)
        for u in range(TC):
            rows = jnp.concatenate([even[8 * u : 8 * u + 8], odd[8 * u : 8 * u + 8]], axis=0)
            f_col[u, pl.ds(pl.multiple_of(m * 16, 16), 16), :] = rows.astype(BF16)

    neighbours = {
        "y": ((r, z * NY + (y + 1) % NY), (r, z * NY + (y + NY - 1) % NY)),
        "z": ((r, ((z + 1) % NZ) * NY + y), (r, ((z + NZ - 1) % NZ) * NY + y)),
    }
    size = {"y": NY, "z": NZ}
    here = {"y": y, "z": z}
    lanes = (pl.ds(0, 128), pl.ds(128, 128))
    full = pl.ds(0, 256)
    def part(g, axis, dest, lane):
        rows = pl.ds(g * PER, PER)
        if KINDS[g] == "A":
            if axis == "y":
                return (rows, slice(None), dest, slice(None), lane)
            return (rows, dest, y, slice(None), lane)
        if axis == "z":
            return (rows, dest, slice(None), slice(None), lane)
        return (rows, z, dest, slice(None), lane)

    def box(g, axis, rnd, way):
        slot = group_slot[g]
        if KINDS[g] == "A":
            first, later = (ay1, ay2) if axis == "y" else (az1, az2)
        else:
            first, later = (bz1, bz2) if axis == "z" else (by1, by2)
        if rnd == 0:
            return first.at[slot, way]
        return later.at[slot, way, rnd - 1]

    def sem_of(g, axis, rnd, way):
        second = axis == ("z" if KINDS[g] == "A" else "y")
        offset = (size["y"] // 2 if KINDS[g] == "A" else size["z"] // 2) if second else 0
        return (g * 6 + offset + rnd) * 2 + way

    def copy_of(g, axis, rnd, way):
        n = size[axis]
        reach = n // 2 - rnd
        sign = 1 if way == 0 else n - 1
        dest = (here[axis] + sign * reach) % n
        lane = lanes[way] if rnd == 0 else full
        k = sem_of(g, axis, rnd, way)
        return pltpu.make_async_remote_copy(
            src_ref=prod.at[part(g, axis, dest, lane)],
            dst_ref=box(g, axis, rnd, way),
            send_sem=rs_send.at[k], recv_sem=rs_recv.at[k],
            device_id=neighbours[axis][way], device_id_type=MESH,
        )

    def take(g, axis, rnd, way):
        n = size[axis]
        reach = n // 2 - rnd - 1
        sign = 1 if way == 0 else n - 1
        dest = (here[axis] + sign * reach) % n
        lane = lanes[way] if rnd == 0 else full
        copy_of(g, axis, rnd, way).wait_recv()
        at = part(g, axis, dest, lane)
        prod[at] = prod[at] + box(g, axis, rnd, way)[...]

    def product(g):
        for t in range(g * PER, g * PER + PER):
            out = jnp.dot(s_rel[t, 0], f_col[0], preferred_element_type=F32)
            for u in range(1, TC):
                out += jnp.dot(s_rel[t, u], f_col[u], preferred_element_type=F32)
            prod[t] = out.reshape(NZ, NY, 8, 256)

    def keep_rows(g):
        slot = group_slot[g]
        span = range(g * PER, g * PER + PER)
        if KINDS[g] == "A":
            for n, piece in enumerate(prod[t, zz, y] for zz in range(NZ) for t in span):
                q_a[slot, n] = piece * (-2.0)
        else:
            for n, piece in enumerate(prod[t, z, yy] for yy in range(NY) for t in span):
                q_b[slot, n] = piece * (-2.0)

    def gather_moment(g):
        slot = group_slot[g]
        if KINDS[g] == "A":
            rows = q_a[slot].reshape(NZ * 16, 256)
            factor = f_z[:, slot * 16 : slot * 16 + 16, :].reshape(NZ * 16, 256)
            weight = near_a[slot]
        else:
            rows = q_b[slot].reshape(NY * 16, 256)
            factor = f_y[:, slot * 16 : slot * 16 + 16, :].reshape(NY * 16, 256)
            weight = near_b[slot]
        pan[...] += jnp.sum((rows * weight).reshape(-1, 8, 256), axis=0)
        flipped = jnp.transpose(factor.astype(F32)).astype(BF16)
        high = rows.astype(BF16)
        rest = rows - high.astype(F32)
        middle = rest.astype(BF16)
        low = (rest - middle.astype(F32)).astype(BF16)
        out = jnp.dot(flipped, low, preferred_element_type=F32)
        out += jnp.dot(flipped, middle, preferred_element_type=F32)
        out += jnp.dot(flipped, high, preferred_element_type=F32)
        mt[...] += out

    def step(g, k):
        axes = ("y", "z") if KINDS[g] == "A" else ("z", "y")
        first = size[axes[0]] // 2
        if k == 0:
            product(g)
            for way in range(2):
                copy_of(g, axes[0], 0, way).start()
            return
        for way in range(2):
            if k <= first:
                take(g, axes[0], k - 1, way)
                if k < first:
                    copy_of(g, axes[0], k, way).start()
            else:
                take(g, axes[1], k - first - 1, way)
                if k < STEPS - 1:
                    copy_of(g, axes[1], k - first, way).start()
        if k == first:
            for way in range(2):
                copy_of(g, axes[1], 0, way).start()
            keep_rows(g)

    def slope_row(t, acc):
        for u in range(TC):
            cross = lax.dot_general(
                u_row[t // 4, t % 4], u_col[u], (((1,), (1,)), ((), ())), preferred_element_type=F32
            )
            across = norm_col[u]
            for k in range(0, 256, 32):
                down = norm_row[t, k : k + 32]
                norms = jnp.concatenate([down, down], axis=1) + across[0:1]
                minus = cross[k : k + 32] * (4.0 * LOG2E / 256.0) - norms
                term = s_rel[t, u, k : k + 32].astype(F32) * (minus * jnp.exp2(minus))
                acc = acc + jnp.sum(term.reshape(4, 8, 256), axis=0)
        return acc

    def ucol_forward():
        return pltpu.make_async_remote_copy(
            src_ref=u_col, dst_ref=u_col,
            send_sem=ucol_send.at[0], recv_sem=ucol_recv,
            device_id=sibling, device_id_type=MESH,
        )

    n_groups = len(KINDS)

    def take_ucol():
        pltpu.make_async_copy(u_col, u_col, ucol_recv).wait()

        @pl.when(feeds)
        def _():
            ucol_forward().start()

        for u in range(TC):
            cols = u_col[u].astype(F32)
            norm = lax.dot_general(
                jnp.ones((8, 256), F32), cols * cols, (((1,), (1,)), ((), ())),
                precision=HIGHEST, preferred_element_type=F32,
            )
            norm_col[u] = norm * (2.0 * LOG2E / 256.0)

    def send_factors():
        for way in range(2):
            fz_to(0, way).start()

        @pl.loop(1, NY)
        def _(d):
            fy_to(d).start()

    def pass_factors(rnd):
        for way in range(2):
            fz_to(rnd - 1, way).wait_recv()
            if rnd + way < 4:
                fz_to(rnd, way).start()

    def take_factors():
        fz_to(3, 0).wait_recv()
        for d in range(1, NY):
            fy_to(d).wait_recv()

    near = []
    for dx in range(NX):
        for dk in range(2):
            for dy in range(NY):
                if dx or dk or dy:
                    near.append((min(dx, NX - dx) + min(dy, NY - dy) + 0.1 * dk, dx, dk, dy))
    near.sort(reverse=True)
    def to_near(stage, src, dst):
        out = []
        for _, dx, dk, dy in near:
            row = xs[dx] + ks[dk]
            out.append(pltpu.make_async_remote_copy(
                src_ref=src(row * NY + ys[dy]), dst_ref=dst,
                send_sem=m_send.at[stage], recv_sem=m_recv.at[stage],
                device_id=(row, z * NY + ys[dy]), device_id_type=MESH,
            ))
        return out

    copies1 = to_near(0, lambda p: m1.at[p], m1r.at[place])
    copies3 = to_near(2, lambda p: m5.at[place], m5.at[place])
    copies2 = [
        pltpu.make_async_remote_copy(
            src_ref=m3.at[z], dst_ref=m3.at[z],
            send_sem=m_send.at[1], recv_sem=m_recv.at[1],
            device_id=(r, ((z + d) % NZ) * NY + y), device_id_type=MESH,
        )
        for d in (4, 3, 5, 2, 6, 1, 7)
    ]

    def wait_all(ref, n, sem):
        blocks = ref.at[pl.ds(0, n)]
        pltpu.make_async_copy(blocks, blocks, sem).wait()

    def sum_first(acc):
        trail = jnp.sum(acc) * (-2.0 / LOG2E / 32768.0)
        panel_part = jnp.sum(pan[...])
        lane = lax.broadcasted_iota(jnp.int32, (8, 256), 1)
        down = lax.broadcasted_iota(jnp.int32, (8, 256), 0)
        for p in range(NR * NY):
            block = jnp.where(jnp.logical_and(down == 7, lane == 0), trail, mt[8 * p : 8 * p + 8])
            m1[p] = jnp.where(jnp.logical_and(down == 7, lane == 1), panel_part, block)
        m1r[place] = m1[place]
        for cp in copies1:
            cp.start()

    def sum_second():
        wait_all(m1r, NR * NY - 1, m_recv.at[0])
        part = m1r[0]
        for j in range(1, NR * NY):
            part = part + m1r[j]
        m3[z] = part
        for cp in copies2:
            cp.start()

    def sum_third():
        wait_all(m3, NZ - 1, m_recv.at[1])
        part = m3[0]
        for j in range(1, NZ):
            part = part + m3[j]
        m5[place] = part
        for cp in copies3:
            cp.start()
        slope_ref[...] = part[7:8, 0:2]

    acc = jnp.zeros((8, 256), F32)
    done = 0
    for event in SCHEDULE:
        if event[0] == "step":
            step(event[1], event[2])
        elif event[0] == "slope":
            acc = lax.fori_loop(done, done + event[1], slope_row, acc)
            done += event[1]
        elif event[0] == "ucol":
            take_ucol()
        elif event[0] == "send":
            send_factors()
        elif event[0] == "pass":
            pass_factors(event[1])
        elif event[0] == "moment":
            gather_moment(event[1])
        elif event[0] == "factors":
            take_factors()
        elif event[0] == "sum1":
            sum_first(acc)
        elif event[0] == "sum2":
            sum_second()

    for t in range(TR):
        total[pl.ds(t * 8, 8), :] = (
            c_ref[pl.ds((t // 2) * 16, 16), :].astype(F32)[(t % 2) * 8 : (t % 2) * 8 + 8]
            - 2.0 * prod[t, z, y]
        )
    adj_ref[...] = jnp.dot(total[...], b_ref[...], precision=HIGHEST, preferred_element_type=F32)
    adj_copy = pltpu.make_async_copy(adj_ref, adj_hbm, in_sem.at[4])
    adj_copy.start()

    sum_third()
    wait_all(m5, NR * NY - 1, m_recv.at[2])
    moment_ref[...] = m5[...]

    adj_copy.wait()
    wait_all(m1r, NR * NY - 1, m_send.at[0])
    wait_all(m3, NZ - 1, m_send.at[1])
    wait_all(m5, NR * NY - 1, m_send.at[2])
    @pl.loop(0, 16)
    def _(n):
        q, xd = far_first(n)
        mine = jnp.logical_and(is_root, jnp.logical_and(q == quarter, xd == x))

        @pl.when(jnp.logical_not(mine))
        def _():
            pltpu.make_async_remote_copy(
                src_ref=f_parts.at[q], dst_ref=f_buf.at[c % 2, c // 2],
                send_sem=f_send.at[n], recv_sem=f_recv.at[0],
                device_id=(2 * xd + c % 2, NR * q + r), device_id_type=MESH,
            ).wait_send()

    @pl.when(feeds)
    def _():
        for d in (1, 2, 3):
            ucol_to(0, d).wait_send()
        ucol_forward().wait_send()

    f_swap.wait_send()
    for rnd in range(4):
        for way in range(2):
            if rnd + way < 4:
                fz_to(rnd, way).wait_send()
    for d in range(1, NY):
        fy_to(d).wait_send()
    for g, kind in enumerate(KINDS):
        for axis in "yz":
            for rnd in range(size[axis] // 2):
                for way in range(2):
                    copy_of(g, axis, rnd, way).wait_send()


def finish(adj_in, m_in, slope_in, b_ref, adj_ref, diag_ref, slope_ref):
    adj_ref[...] = adj_in[...]
    slope_ref[...] = slope_in[...]
    diag = lax.dot_general(
        b_ref[...], m_in[...], (((0,), (1,)), ((), ())),
        precision=HIGHEST, preferred_element_type=F32,
    )
    down = lax.broadcasted_iota(jnp.int32, (256, 256), 0)
    across = lax.broadcasted_iota(jnp.int32, (256, 256), 1)
    diag_ref[...] = jnp.where(down >= across, -diag, 0.0)


def local(trailing_cot, panel_factor, panel_cot, block_inverse, row_desc, panel_desc):
    s_rows = trailing_cot.reshape(TR, 256, TC, 2, 128).transpose(0, 1, 3, 2, 4).reshape(TR * 2048, 128)
    hbm = pl.BlockSpec(memory_space=pl.ANY)
    vmem = pl.BlockSpec(memory_space=pltpu.VMEM)
    dma = pltpu.SemaphoreType.DMA
    V = pltpu.VMEM
    adjoint, moment, slope = pl.pallas_call(
        kernel,
        out_shape=(
            jax.ShapeDtypeStruct((128, 256), F32),
            jax.ShapeDtypeStruct((NR * NY, 8, 256), F32),
            jax.ShapeDtypeStruct((1, 2), F32),
        ),
        in_specs=[hbm] * 6,
        out_specs=(hbm, vmem, vmem),
        scratch_shapes=[
            V((128, 256), BF16),
            V((128, 256), BF16),
            V((256, 256), F32),
            V((256, 256), BF16),
            V((128, 256), F32),
            V((TR, 2048, 128), BF16),
            V((2048, 128), F32),
            V((TR, TC, 256, 256), BF16),
            V((4, 4, 256, 256), BF16),
            V((TC, 256, 256), BF16),
            V((TR, 256, 128), F32),
            V((TC, 8, 256), F32),
            V((4, 32, 256), BF16),
            V((2, 16, 32, 256), BF16),
            V((TC, 256, 256), BF16),
            V((NZ, N_A * 16, 256), BF16),
            V((NY, N_B * 16, 256), BF16),
            V((TR, NZ, NY, 8, 256), F32),
            V((128, 256), F32),
            V((N_A, NZ * 16, 256), F32),
            V((N_B, NY * 16, 256), F32),
            V((N_A, NZ * 2, 8, 256), F32),
            V((N_B, NY * 2, 8, 256), F32),
            V((256, 256), F32),
            V((8, 256), F32),
            V((N_A, 2, PER, NZ, 8, 128), F32),
            V((N_A, 2, 1, PER, NZ, 8, 256), F32),
            V((N_A, 2, PER, 8, 128), F32),
            V((N_A, 2, 3, PER, 8, 256), F32),
            V((N_B, 2, PER, NY, 8, 128), F32),
            V((N_B, 2, 3, PER, NY, 8, 256), F32),
            V((N_B, 2, PER, 8, 128), F32),
            V((N_B, 2, 1, PER, 8, 256), F32),
            V((NR * NY, 8, 256), F32),
            V((NR * NY, 8, 256), F32),
            V((NZ, 8, 256), F32),
            V((NR * NY, 8, 256), F32),
            dma((TR,)),
            dma((5,)),
            dma,
            dma((16,)),
            dma((2,)),
            dma,
            dma((NZ + NY,)),
            dma((NZ + NY,)),
            dma((4,)),
            dma,
            dma((len(KINDS) * 12,)),
            dma((len(KINDS) * 12,)),
            dma((3,)),
            dma((3,)),
        ],
        compiler_params=pltpu.CompilerParams(
            collective_id=0, has_side_effects=True, vmem_limit_bytes=60 * 1024 * 1024
        ),
        cost_estimate=pl.CostEstimate(
            flops=4 * 4096 * 1024 * 256, bytes_accessed=12 * 1024 * 1024, transcendentals=4096 * 1024
        ),
        name="panel_step",
    )(
        row_desc.reshape(4, 4, 256, 256),
        s_rows,
        panel_cot.reshape(128, 256),
        panel_factor.reshape(128, 256),
        block_inverse,
        panel_desc,
    )
    adjoint, diag, slope = pl.pallas_call(
        finish,
        out_shape=(
            jax.ShapeDtypeStruct((128, 256), F32),
            jax.ShapeDtypeStruct((256, 256), F32),
            jax.ShapeDtypeStruct((1, 2), F32),
        ),
        in_specs=[vmem] * 4,
        out_specs=(vmem, vmem, vmem),
        name="finish",
    )(adjoint, moment.reshape(256, 256), slope, block_inverse)
    return adjoint.reshape(16, 8, 256), diag, slope.reshape(2)


def solution(mesh):
    in_specs = (
        P(None, "row", None, "col"),
        P(None, ("row", "col"), None),
        P(None, ("row", "col"), None),
        P(),
        P(None, "row", None),
        P(),
    )
    out_specs = (P(None, ("row", "col"), None), P(), P())
    return jax.shard_map(local, mesh=mesh, in_specs=in_specs, out_specs=out_specs, check_vma=False)
```

```python
import functools
import math

import jax
import jax.numpy as jnp
from jax import lax
from jax.experimental import pallas as pl
from jax.experimental.pallas import tpu as pltpu
from jax.sharding import PartitionSpec as P

MESH = pl.DeviceIdType.MESH
HIGHEST = lax.Precision.HIGHEST
F32 = jnp.float32
BF16 = jnp.bfloat16
LOG2E = math.log2(math.e)

TR = 16
TC = 4
NX, NY, NZ, NR = 4, 4, 8, 8
PER = 2
KINDS = "ABABABAB"
N_A = KINDS.count("A")
N_B = KINDS.count("B")
EARLY = 3
STEPS = 7


SCHEDULE = [
    ("send",), ("step", 7, 0), ("step", 3, 0), ("step", 5, 0), ("step", 1, 0), ("step", 6, 0), ("step", 7, 1),
    ("step", 2, 0), ("step", 3, 1), ("pass", 1), ("step", 4, 0), ("upass",), ("step", 5, 1), ("step", 1, 1),
    ("step", 0, 0), ("ucol",), ("slope", 1), ("step", 6, 1), ("step", 7, 2), ("slope", 1), ("pass", 2),
    ("slope", 1), ("step", 2, 1), ("step", 3, 2), ("slope", 1), ("slope", 1), ("step", 4, 1), ("step", 5, 2),
    ("slope", 1), ("pass", 3), ("slope", 1), ("step", 0, 1), ("step", 1, 2), ("slope", 1), ("slope", 1),
    ("step", 7, 3), ("slope", 1), ("slope", 1), ("step", 6, 2), ("step", 3, 3), ("factors",), ("moment", 6),
    ("slope", 1), ("slope", 1), ("step", 5, 3), ("slope", 1), ("slope", 1), ("step", 2, 2), ("step", 1, 3),
    ("moment", 2), ("slope", 1), ("step", 7, 4), ("step", 6, 3), ("moment", 7), ("step", 4, 2), ("moment", 4),
    ("step", 3, 4), ("moment", 3), ("step", 5, 4), ("step", 2, 3), ("moment", 5), ("step", 0, 2),
    ("step", 7, 5), ("moment", 0), ("step", 1, 4), ("step", 6, 4), ("step", 4, 3), ("step", 3, 5),
    ("moment", 1), ("sum1",), ("step", 2, 4), ("step", 0, 3), ("step", 5, 5), ("step", 7, 6), ("step", 1, 5),
    ("step", 6, 5), ("step", 4, 4), ("step", 3, 6), ("step", 2, 5), ("step", 0, 4), ("sum2",), ("step", 5, 6),
    ("step", 1, 6), ("step", 6, 6), ("step", 4, 5), ("step", 2, 6), ("step", 0, 5), ("step", 4, 6),
    ("step", 0, 6),
]


def kernel(
    u_hbm, s_hbm, c_hbm, f_hbm, b_hbm, pd_hbm,
    adj_hbm, moment_ref, slope_ref,
    c_ref, f_own, b_ref, pd_ref, adj_ref,
    s_raw, s_f32, s_rel, u_row, u_col, norm_row, norm_col, f_parts, f_buf, f_col, f_z, f_y, prod, total, near_a, near_b, q_a, q_b, mt, pan,
    ay1, ay2, az1, az2, bz1, bz2, by1, by2,
    m1, m1r, m3, m5,
    s_sem, in_sem, u_sem, f_send, f_recv, f_local, fz_send, fz_recv, ucol_send, ucol_recv, rs_send, rs_recv, m_send, m_recv,
):
    r = lax.axis_index("row")
    c = lax.axis_index("col")
    x, core = r // 2, r % 2
    z, y = c // NY, c % NY
    root = c % NR
    quarter = c // NR
    is_root = root == r
    feeds = core == y % 2
    place = r * NY + y

    def near_dev(p):
        return (p // NY, z * NY + p % NY)

    def partner(u):
        side = z + 1 - 2 * (z % 2) if u // 2 else z
        return side * NY + (y + 2 * (u % 2)) % NY

    barrier = pltpu.get_barrier_semaphore()

    def greet(dev):
        pl.semaphore_signal(barrier, inc=1, device_id=dev, device_id_type=MESH)

    @pl.loop(0, 16)
    def _(m):
        @pl.when(jnp.logical_not(jnp.logical_and(is_root, 2 * m + core == c)))
        def _():
            greet((root, 2 * m + core))

    @pl.when(jnp.logical_and(feeds, jnp.logical_not(is_root)))
    def _():
        for u in range(TC):
            greet((root, partner(u)))

    xs = [((x + d) % NX) * 2 for d in range(NX)]
    ks = [core, 1 - core]
    ys = [(y + d) % NY for d in range(NY)]
    for dx in (2, 1, 3, 0):
        for dy in (2, 1, 3, 0):
            for dk in range(2):
                if dx or dk or dy:
                    greet((xs[dx] + ks[dk], z * NY + ys[dy]))

    @pl.loop(1, NZ)
    def _(d):
        greet((r, ((z + d) % NZ) * NY + y))

    s_copies = [
        pltpu.make_async_copy(s_hbm.at[pl.ds(t * 2048, 2048)], s_raw.at[t], s_sem.at[t])
        for t in range(TR)
    ]
    u_copy = pltpu.make_async_copy(u_hbm, u_row, u_sem)
    f_copy = pltpu.make_async_copy(f_hbm, f_own, in_sem.at[0])
    small = [
        pltpu.make_async_copy(c_hbm, c_ref, in_sem.at[1]),
        pltpu.make_async_copy(b_hbm, b_ref, in_sem.at[2]),
        pltpu.make_async_copy(pd_hbm, pd_ref, in_sem.at[3]),
    ]
    f_copy.start()
    for cp in s_copies[:2]:
        cp.start()
    u_copy.start()
    for cp in small:
        cp.start()
    for cp in s_copies[2:]:
        cp.start()

    f_copy.wait()
    f_wide = f_own[...].astype(F32)
    for q in range(4):
        f_parts[q] = jnp.concatenate(
            [f_wide[(4 * u + q) * 8 : (4 * u + q) * 8 + 8] for u in range(TC)], axis=0
        ).astype(BF16)

    for kind, store in (("A", f_z.at[z]), ("B", f_y.at[y])):
        for slot, g in enumerate(n for n, k in enumerate(KINDS) if k == kind):
            store[slot * 16 : slot * 16 + 16, :] = f_own[g * 16 : g * 16 + 16, :]

    def relay(t):
        s_f32[...] = s_raw[t].astype(F32)
        for u in range(TC):
            for half in range(2):
                s_rel[t, u, :, half * 128 : half * 128 + 128] = s_f32[
                    pl.ds(half * 4 + u, 256, stride=8), :
                ].astype(BF16)

    for t in range(EARLY):
        s_copies[t].wait()

    @pl.loop(0, EARLY)
    def _(t):
        relay(t)

    pl.semaphore_wait(barrier, 16 + 31 + 7 - jnp.where(is_root, 1, 0) + jnp.where(feeds, 3, 0))

    def rows_to(dq, dx):
        q = (z // 2 + dq) % 4
        return pltpu.make_async_remote_copy(
            src_ref=f_parts.at[q], dst_ref=f_buf.at[c % 2, c // 2],
            send_sem=f_send.at[NX * dq + dx], recv_sem=f_recv.at[0],
            device_id=(xs[dx] + c % 2, NR * q + r), device_id_type=MESH,
        )

    for dq in (2, 1, 3, 0):
        for dx in (2, 1, 3, 0):
            if dq or dx:
                rows_to(dq, dx).start()

    @pl.when(is_root)
    def _():
        pltpu.make_async_copy(f_parts.at[quarter], f_buf.at[c % 2, c // 2], f_recv.at[0]).start()

    @pl.when(jnp.logical_not(is_root))
    def _():
        rows_to(0, 0).start()

    def ucol_to(u, d):
        return pltpu.make_async_remote_copy(
            src_ref=u_hbm.at[u, quarter], dst_ref=u_col.at[u],
            send_sem=ucol_send.at[d], recv_sem=ucol_recv,
            device_id=(((x + d) % NX) * 2 + core, partner(u)), device_id_type=MESH,
        )

    def send_ucol():
        for u in range(TC):
            @pl.when(partner(u) % NR == r)
            def _():
                for d in (2, 1, 3):
                    ucol_to(u, d).start()

        @pl.when(is_root)
        def _():
            pltpu.make_async_copy(u_hbm.at[:, quarter], u_col, ucol_recv).start()

    send_ucol()

    def fz_to(rnd, way):
        sign = 1 if way == 0 else NZ - 1
        held = (z + (NZ - sign) * rnd) % NZ
        return pltpu.make_async_remote_copy(
            src_ref=f_z.at[held], dst_ref=f_z.at[held],
            send_sem=fz_send.at[4 * way + rnd], recv_sem=fz_recv.at[4 * way + rnd],
            device_id=(r, ((z + sign) % NZ) * NY + y), device_id_type=MESH,
        )

    def fy_to(d):
        return pltpu.make_async_remote_copy(
            src_ref=f_y.at[y], dst_ref=f_y.at[y],
            send_sem=fz_send.at[NZ + d], recv_sem=fz_recv.at[NZ + d],
            device_id=(r, z * NY + (y + d) % NY), device_id_type=MESH,
        )

    for t in range(EARLY, TR):
        s_copies[t].wait()

    @pl.loop(EARLY, TR)
    def _(t):
        relay(t)

    u_copy.wait()
    for cp in small:
        cp.wait()

    @pl.loop(0, TR)
    def _(t):
        rows = u_row[t // 4, t % 4].astype(F32)
        norm = jnp.sum(rows * rows, axis=-1, keepdims=True) * (2.0 * LOG2E / 256.0)
        norm_row[t] = jnp.broadcast_to(norm, (256, 128))

    panel = pd_ref[...].astype(F32)
    panel_norm = lax.dot_general(
        jnp.ones((8, 256), F32), panel * panel, (((1,), (1,)), ((), ())),
        precision=HIGHEST, preferred_element_type=F32,
    )

    def weights(rows):
        norm = jnp.sum(rows * rows, axis=-1, keepdims=True)
        cross = lax.dot_general(
            rows.astype(BF16), pd_ref[...], (((1,), (1,)), ((), ())), preferred_element_type=F32
        )
        scaled = (2.0 / 256.0) * (norm + panel_norm[0:1] - 2.0 * cross)
        weight = 2.0 * scaled * jnp.exp(-scaled) * (1.0 / math.sqrt(8388608))
        return lax.dot_general(
            weight, b_ref[...], (((1,), (1,)), ((), ())),
            precision=HIGHEST, preferred_element_type=F32,
        )

    group_slot = {}
    for g, kind in enumerate(KINDS):
        group_slot[g] = KINDS[:g].count(kind)
    pan[...] = jnp.zeros((8, 256), F32)
    for g, kind in enumerate(KINDS):
        slot = group_slot[g]
        rows = []
        if kind == "A":
            for zz in range(NZ):
                for t in range(g * PER, g * PER + PER):
                    first = pl.multiple_of(zz * 32 + (y // 2) * 16, 16)
                    pair = u_row[t // 4, t % 4, pl.ds(first, 16), :].astype(F32)
                    rows.append(jnp.where(y % 2 == 0, pair[0:8], pair[8:16]))
            near, mine = near_a, z
        else:
            wide = [
                u_row[t // 4, t % 4, pl.ds(pl.multiple_of(z * 32, 32), 32), :].astype(F32)
                for t in range(g * PER, g * PER + PER)
            ]
            for yy in range(NY):
                for w in wide:
                    rows.append(w[yy * 8 : yy * 8 + 8])
            near, mine = near_b, y
        near[slot] = weights(jnp.concatenate(rows, axis=0))
        own_c = c_ref[g * 16 : g * 16 + 16, :].astype(F32)
        own_w = near[slot, pl.ds(pl.multiple_of(mine * 16, 16), 16), :]
        pan[...] += jnp.sum((own_c * own_w).reshape(2, 8, 256), axis=0)
    mt[...] = lax.dot_general(
        f_own[...], c_ref[...], (((0,), (0,)), ((), ())), preferred_element_type=F32
    )

    sibling = (2 * x + 1 - core, c)

    pltpu.make_async_copy(f_buf.at[0], f_buf.at[0], f_recv.at[0]).wait()
    f_swap = pltpu.make_async_remote_copy(
        src_ref=f_buf.at[core], dst_ref=f_buf.at[core],
        send_sem=f_local, recv_sem=f_recv.at[1],
        device_id=sibling, device_id_type=MESH,
    )
    f_swap.start()

    f_swap.wait_recv()

    @pl.loop(0, 16, unroll=4)
    def _(m):
        even = f_buf[0, m].astype(F32)
        odd = f_buf[1, m].astype(F32)
        for u in range(TC):
            rows = jnp.concatenate([even[8 * u : 8 * u + 8], odd[8 * u : 8 * u + 8]], axis=0)
            f_col[u, pl.ds(pl.multiple_of(m * 16, 16), 16), :] = rows.astype(BF16)

    neighbours = {
        "y": ((r, z * NY + (y + 1) % NY), (r, z * NY + (y + NY - 1) % NY)),
        "z": ((r, ((z + 1) % NZ) * NY + y), (r, ((z + NZ - 1) % NZ) * NY + y)),
    }
    size = {"y": NY, "z": NZ}
    here = {"y": y, "z": z}
    lanes = (pl.ds(0, 128), pl.ds(128, 128))
    full = pl.ds(0, 256)
    def part(g, axis, dest, lane):
        rows = pl.ds(g * PER, PER)
        if KINDS[g] == "A":
            if axis == "y":
                return (rows, slice(None), dest, slice(None), lane)
            return (rows, dest, y, slice(None), lane)
        if axis == "z":
            return (rows, dest, slice(None), slice(None), lane)
        return (rows, z, dest, slice(None), lane)

    def box(g, axis, rnd, way):
        slot = group_slot[g]
        if KINDS[g] == "A":
            first, later = (ay1, ay2) if axis == "y" else (az1, az2)
        else:
            first, later = (bz1, bz2) if axis == "z" else (by1, by2)
        if rnd == 0:
            return first.at[slot, way]
        return later.at[slot, way, rnd - 1]

    def sem_of(g, axis, rnd, way):
        second = axis == ("z" if KINDS[g] == "A" else "y")
        offset = (size["y"] // 2 if KINDS[g] == "A" else size["z"] // 2) if second else 0
        return (g * 6 + offset + rnd) * 2 + way

    def copy_of(g, axis, rnd, way):
        n = size[axis]
        reach = n // 2 - rnd
        sign = 1 if way == 0 else n - 1
        dest = (here[axis] + sign * reach) % n
        lane = lanes[way] if rnd == 0 else full
        k = sem_of(g, axis, rnd, way)
        return pltpu.make_async_remote_copy(
            src_ref=prod.at[part(g, axis, dest, lane)],
            dst_ref=box(g, axis, rnd, way),
            send_sem=rs_send.at[k], recv_sem=rs_recv.at[k],
            device_id=neighbours[axis][way], device_id_type=MESH,
        )

    def take(g, axis, rnd, way):
        n = size[axis]
        reach = n // 2 - rnd - 1
        sign = 1 if way == 0 else n - 1
        dest = (here[axis] + sign * reach) % n
        lane = lanes[way] if rnd == 0 else full
        copy_of(g, axis, rnd, way).wait_recv()
        at = part(g, axis, dest, lane)
        prod[at] = prod[at] + box(g, axis, rnd, way)[...]

    def product(g):
        for t in range(g * PER, g * PER + PER):
            out = jnp.dot(s_rel[t, 0], f_col[0], preferred_element_type=F32)
            for u in range(1, TC):
                out += jnp.dot(s_rel[t, u], f_col[u], preferred_element_type=F32)
            prod[t] = out.reshape(NZ, NY, 8, 256)

    def keep_rows(g):
        slot = group_slot[g]
        span = range(g * PER, g * PER + PER)
        if KINDS[g] == "A":
            for n, piece in enumerate(prod[t, zz, y] for zz in range(NZ) for t in span):
                q_a[slot, n] = piece * (-2.0)
        else:
            for n, piece in enumerate(prod[t, z, yy] for yy in range(NY) for t in span):
                q_b[slot, n] = piece * (-2.0)

    def gather_moment(g):
        slot = group_slot[g]
        if KINDS[g] == "A":
            rows = q_a[slot].reshape(NZ * 16, 256)
            factor = f_z[:, slot * 16 : slot * 16 + 16, :].reshape(NZ * 16, 256)
            weight = near_a[slot]
        else:
            rows = q_b[slot].reshape(NY * 16, 256)
            factor = f_y[:, slot * 16 : slot * 16 + 16, :].reshape(NY * 16, 256)
            weight = near_b[slot]
        pan[...] += jnp.sum((rows * weight).reshape(-1, 8, 256), axis=0)
        flipped = jnp.transpose(factor.astype(F32)).astype(BF16)
        high = rows.astype(BF16)
        rest = rows - high.astype(F32)
        middle = rest.astype(BF16)
        low = (rest - middle.astype(F32)).astype(BF16)
        out = jnp.dot(flipped, low, preferred_element_type=F32)
        out += jnp.dot(flipped, middle, preferred_element_type=F32)
        out += jnp.dot(flipped, high, preferred_element_type=F32)
        mt[...] += out

    def step(g, k):
        axes = ("y", "z") if KINDS[g] == "A" else ("z", "y")
        first = size[axes[0]] // 2
        if k == 0:
            product(g)
            for way in range(2):
                copy_of(g, axes[0], 0, way).start()
            return
        for way in range(2):
            if k <= first:
                take(g, axes[0], k - 1, way)
                if k < first:
                    copy_of(g, axes[0], k, way).start()
            else:
                take(g, axes[1], k - first - 1, way)
                if k < STEPS - 1:
                    copy_of(g, axes[1], k - first, way).start()
        if k == first:
            for way in range(2):
                copy_of(g, axes[1], 0, way).start()
            keep_rows(g)

    def slope_row(t, acc):
        for u in range(TC):
            cross = lax.dot_general(
                u_row[t // 4, t % 4], u_col[u], (((1,), (1,)), ((), ())), preferred_element_type=F32
            )
            across = norm_col[u]
            for k in range(0, 256, 32):
                down = norm_row[t, k : k + 32]
                norms = jnp.concatenate([down, down], axis=1) + across[0:1]
                minus = cross[k : k + 32] * (4.0 * LOG2E / 256.0) - norms
                term = s_rel[t, u, k : k + 32].astype(F32) * (minus * jnp.exp2(minus))
                acc = acc + jnp.sum(term.reshape(4, 8, 256), axis=0)
        return acc

    def ucol_forward():
        return pltpu.make_async_remote_copy(
            src_ref=u_col, dst_ref=u_col,
            send_sem=ucol_send.at[0], recv_sem=ucol_recv,
            device_id=sibling, device_id_type=MESH,
        )

    n_groups = len(KINDS)

    def take_ucol():
        pltpu.make_async_copy(u_col, u_col, ucol_recv).wait()

        @pl.when(feeds)
        def _():
            ucol_forward().start()

        for u in range(TC):
            cols = u_col[u].astype(F32)
            norm = lax.dot_general(
                jnp.ones((8, 256), F32), cols * cols, (((1,), (1,)), ((), ())),
                precision=HIGHEST, preferred_element_type=F32,
            )
            norm_col[u] = norm * (2.0 * LOG2E / 256.0)

    def send_factors():
        for way in range(2):
            fz_to(0, way).start()

        @pl.loop(1, NY)
        def _(d):
            fy_to(d).start()

    def pass_factors(rnd):
        for way in range(2):
            fz_to(rnd - 1, way).wait_recv()
            if rnd + way < 4:
                fz_to(rnd, way).start()

    def take_factors():
        fz_to(3, 0).wait_recv()
        for d in range(1, NY):
            fy_to(d).wait_recv()

    near = []
    for dx in range(NX):
        for dk in range(2):
            for dy in range(NY):
                if dx or dk or dy:
                    near.append((min(dx, NX - dx) + min(dy, NY - dy) + 0.1 * dk, dx, dk, dy))
    near.sort(reverse=True)
    def to_near(stage, src, dst):
        out = []
        for _, dx, dk, dy in near:
            row = xs[dx] + ks[dk]
            out.append(pltpu.make_async_remote_copy(
                src_ref=src(row * NY + ys[dy]), dst_ref=dst,
                send_sem=m_send.at[stage], recv_sem=m_recv.at[stage],
                device_id=(row, z * NY + ys[dy]), device_id_type=MESH,
            ))
        return out

    copies1 = to_near(0, lambda p: m1.at[p], m1r.at[place])
    copies3 = to_near(2, lambda p: m5.at[place], m5.at[place])
    copies2 = [
        pltpu.make_async_remote_copy(
            src_ref=m3.at[z], dst_ref=m3.at[z],
            send_sem=m_send.at[1], recv_sem=m_recv.at[1],
            device_id=(r, ((z + d) % NZ) * NY + y), device_id_type=MESH,
        )
        for d in (4, 3, 5, 2, 6, 1, 7)
    ]

    def wait_all(ref, n, sem):
        blocks = ref.at[pl.ds(0, n)]
        pltpu.make_async_copy(blocks, blocks, sem).wait()

    def sum_first(acc):
        trail = jnp.sum(acc) * (-2.0 / LOG2E / 32768.0)
        panel_part = jnp.sum(pan[...])
        lane = lax.broadcasted_iota(jnp.int32, (8, 256), 1)
        down = lax.broadcasted_iota(jnp.int32, (8, 256), 0)
        for p in range(NR * NY):
            block = jnp.where(jnp.logical_and(down == 7, lane == 0), trail, mt[8 * p : 8 * p + 8])
            m1[p] = jnp.where(jnp.logical_and(down == 7, lane == 1), panel_part, block)
        m1r[place] = m1[place]
        for cp in copies1:
            cp.start()

    def sum_second():
        wait_all(m1r, NR * NY - 1, m_recv.at[0])
        part = m1r[0]
        for j in range(1, NR * NY):
            part = part + m1r[j]
        m3[z] = part
        for cp in copies2:
            cp.start()

    def sum_third():
        wait_all(m3, NZ - 1, m_recv.at[1])
        part = m3[0]
        for j in range(1, NZ):
            part = part + m3[j]
        m5[place] = part
        for cp in copies3:
            cp.start()
        slope_ref[...] = part[7:8, 0:2]

    acc = jnp.zeros((8, 256), F32)
    done = 0
    for event in SCHEDULE:
        if event[0] == "step":
            step(event[1], event[2])
        elif event[0] == "slope":
            acc = lax.fori_loop(done, done + event[1], slope_row, acc)
            done += event[1]
        elif event[0] == "ucol":
            take_ucol()
        elif event[0] == "send":
            send_factors()
        elif event[0] == "pass":
            pass_factors(event[1])
        elif event[0] == "moment":
            gather_moment(event[1])
        elif event[0] == "factors":
            take_factors()
        elif event[0] == "sum1":
            sum_first(acc)
        elif event[0] == "sum2":
            sum_second()

    for t in range(TR):
        total[pl.ds(t * 8, 8), :] = (
            c_ref[pl.ds((t // 2) * 16, 16), :].astype(F32)[(t % 2) * 8 : (t % 2) * 8 + 8]
            - 2.0 * prod[t, z, y]
        )
    adj_ref[...] = jnp.dot(total[...], b_ref[...], precision=HIGHEST, preferred_element_type=F32)
    adj_copy = pltpu.make_async_copy(adj_ref, adj_hbm, in_sem.at[4])
    adj_copy.start()

    sum_third()
    adj_copy.wait()
    wait_all(m1r, NR * NY - 1, m_send.at[0])
    wait_all(m3, NZ - 1, m_send.at[1])
    for dq in range(4):
        for dx in range(NX):
            if dq or dx:
                rows_to(dq, dx).wait_send()

    @pl.when(jnp.logical_not(is_root))
    def _():
        rows_to(0, 0).wait_send()

    @pl.when(feeds)
    def _():
        for d in (1, 2, 3):
            ucol_to(0, d).wait_send()
        ucol_forward().wait_send()

    f_swap.wait_send()
    for rnd in range(4):
        for way in range(2):
            if rnd + way < 4:
                fz_to(rnd, way).wait_send()
    for d in range(1, NY):
        fy_to(d).wait_send()
    for g, kind in enumerate(KINDS):
        for axis in "yz":
            for rnd in range(size[axis] // 2):
                for way in range(2):
                    copy_of(g, axis, rnd, way).wait_send()

    wait_all(m5, NR * NY - 1, m_recv.at[2])
    moment_ref[...] = m5[...]
    wait_all(m5, NR * NY - 1, m_send.at[2])

def finish(adj_in, m_in, slope_in, b_ref, adj_ref, diag_ref, slope_ref):
    adj_ref[...] = adj_in[...]
    slope_ref[...] = slope_in[...]
    diag = lax.dot_general(
        b_ref[...], m_in[...], (((0,), (1,)), ((), ())),
        precision=HIGHEST, preferred_element_type=F32,
    )
    down = lax.broadcasted_iota(jnp.int32, (256, 256), 0)
    across = lax.broadcasted_iota(jnp.int32, (256, 256), 1)
    diag_ref[...] = jnp.where(down >= across, -diag, 0.0)


def local(trailing_cot, panel_factor, panel_cot, block_inverse, row_desc, panel_desc):
    s_rows = trailing_cot.reshape(TR, 256, TC, 2, 128).transpose(0, 1, 3, 2, 4).reshape(TR * 2048, 128)
    hbm = pl.BlockSpec(memory_space=pl.ANY)
    vmem = pl.BlockSpec(memory_space=pltpu.VMEM)
    dma = pltpu.SemaphoreType.DMA
    V = pltpu.VMEM
    adjoint, moment, slope = pl.pallas_call(
        kernel,
        out_shape=(
            jax.ShapeDtypeStruct((128, 256), F32),
            jax.ShapeDtypeStruct((NR * NY, 8, 256), F32),
            jax.ShapeDtypeStruct((1, 2), F32),
        ),
        in_specs=[hbm] * 6,
        out_specs=(hbm, vmem, vmem),
        scratch_shapes=[
            V((128, 256), BF16),
            V((128, 256), BF16),
            V((256, 256), F32),
            V((256, 256), BF16),
            V((128, 256), F32),
            V((TR, 2048, 128), BF16),
            V((2048, 128), F32),
            V((TR, TC, 256, 256), BF16),
            V((4, 4, 256, 256), BF16),
            V((TC, 256, 256), BF16),
            V((TR, 256, 128), F32),
            V((TC, 8, 256), F32),
            V((4, 32, 256), BF16),
            V((2, 16, 32, 256), BF16),
            V((TC, 256, 256), BF16),
            V((NZ, N_A * 16, 256), BF16),
            V((NY, N_B * 16, 256), BF16),
            V((TR, NZ, NY, 8, 256), F32),
            V((128, 256), F32),
            V((N_A, NZ * 16, 256), F32),
            V((N_B, NY * 16, 256), F32),
            V((N_A, NZ * 2, 8, 256), F32),
            V((N_B, NY * 2, 8, 256), F32),
            V((256, 256), F32),
            V((8, 256), F32),
            V((N_A, 2, PER, NZ, 8, 128), F32),
            V((N_A, 2, 1, PER, NZ, 8, 256), F32),
            V((N_A, 2, PER, 8, 128), F32),
            V((N_A, 2, 3, PER, 8, 256), F32),
            V((N_B, 2, PER, NY, 8, 128), F32),
            V((N_B, 2, 3, PER, NY, 8, 256), F32),
            V((N_B, 2, PER, 8, 128), F32),
            V((N_B, 2, 1, PER, 8, 256), F32),
            V((NR * NY, 8, 256), F32),
            V((NR * NY, 8, 256), F32),
            V((NZ, 8, 256), F32),
            V((NR * NY, 8, 256), F32),
            dma((TR,)),
            dma((5,)),
            dma,
            dma((16,)),
            dma((2,)),
            dma,
            dma((NZ + NY,)),
            dma((NZ + NY,)),
            dma((4,)),
            dma,
            dma((len(KINDS) * 12,)),
            dma((len(KINDS) * 12,)),
            dma((3,)),
            dma((3,)),
        ],
        compiler_params=pltpu.CompilerParams(
            collective_id=0, has_side_effects=True, vmem_limit_bytes=60 * 1024 * 1024
        ),
        cost_estimate=pl.CostEstimate(
            flops=4 * 4096 * 1024 * 256, bytes_accessed=12 * 1024 * 1024, transcendentals=4096 * 1024
        ),
        name="panel_step",
    )(
        row_desc.reshape(4, 4, 256, 256),
        s_rows,
        panel_cot.reshape(128, 256),
        panel_factor.reshape(128, 256),
        block_inverse,
        panel_desc,
    )
    adjoint, diag, slope = pl.pallas_call(
        finish,
        out_shape=(
            jax.ShapeDtypeStruct((128, 256), F32),
            jax.ShapeDtypeStruct((256, 256), F32),
            jax.ShapeDtypeStruct((1, 2), F32),
        ),
        in_specs=[vmem] * 4,
        out_specs=(vmem, vmem, vmem),
        name="finish",
    )(adjoint, moment.reshape(256, 256), slope, block_inverse)
    return adjoint.reshape(16, 8, 256), diag, slope.reshape(2)


def solution(mesh):
    in_specs = (
        P(None, "row", None, "col"),
        P(None, ("row", "col"), None),
        P(None, ("row", "col"), None),
        P(),
        P(None, "row", None),
        P(),
    )
    out_specs = (P(None, ("row", "col"), None), P(), P())
    return jax.shard_map(local, mesh=mesh, in_specs=in_specs, out_specs=out_specs, check_vma=False)
```

```python
import functools
import math

import jax
import jax.numpy as jnp
from jax import lax
from jax.experimental import pallas as pl
from jax.experimental.pallas import tpu as pltpu
from jax.sharding import PartitionSpec as P

MESH = pl.DeviceIdType.MESH
HIGHEST = lax.Precision.HIGHEST
F32 = jnp.float32
BF16 = jnp.bfloat16
LOG2E = math.log2(math.e)

TR = 16
TC = 4
NX, NY, NZ, NR = 4, 4, 8, 8
PER = 2
KINDS = "ABABABAB"
N_A = KINDS.count("A")
N_B = KINDS.count("B")
EARLY = 3
STEPS = 7


SCHEDULE = [
    ("send",), ("step", 7, 0), ("step", 3, 0), ("step", 5, 0), ("step", 1, 0), ("step", 6, 0), ("step", 7, 1),
    ("step", 2, 0), ("step", 3, 1), ("pass", 1), ("step", 4, 0), ("upass",), ("step", 5, 1), ("step", 1, 1),
    ("step", 0, 0), ("ucol",), ("slope", 1), ("step", 6, 1), ("step", 7, 2), ("slope", 1), ("pass", 2),
    ("slope", 1), ("step", 2, 1), ("step", 3, 2), ("slope", 1), ("slope", 1), ("step", 4, 1), ("step", 5, 2),
    ("slope", 1), ("pass", 3), ("slope", 1), ("step", 0, 1), ("step", 1, 2), ("slope", 1), ("slope", 1),
    ("step", 7, 3), ("slope", 1), ("slope", 1), ("step", 6, 2), ("step", 3, 3), ("factors",), ("moment", 6),
    ("slope", 1), ("slope", 1), ("step", 5, 3), ("slope", 1), ("slope", 1), ("step", 2, 2), ("step", 1, 3),
    ("moment", 2), ("slope", 1), ("step", 7, 4), ("step", 6, 3), ("moment", 7), ("step", 4, 2), ("moment", 4),
    ("step", 3, 4), ("moment", 3), ("step", 5, 4), ("step", 2, 3), ("moment", 5), ("step", 0, 2),
    ("step", 7, 5), ("moment", 0), ("step", 1, 4), ("step", 6, 4), ("step", 4, 3), ("step", 3, 5),
    ("moment", 1), ("sum1",), ("step", 2, 4), ("step", 0, 3), ("step", 5, 5), ("step", 7, 6), ("step", 1, 5),
    ("step", 6, 5), ("step", 4, 4), ("step", 3, 6), ("step", 2, 5), ("step", 0, 4), ("sum2",), ("step", 5, 6),
    ("step", 1, 6), ("step", 6, 6), ("step", 4, 5), ("step", 2, 6), ("step", 0, 5), ("step", 4, 6),
    ("step", 0, 6),
]


def kernel(
    u_hbm, s_hbm, c_hbm, f_hbm, b_hbm, pd_hbm,
    adj_hbm, moment_ref, slope_ref,
    c_ref, f_own, b_ref, pd_ref, adj_ref,
    s_raw, s_f32, s_rel, u_row, u_col, norm_row, norm_col, f_parts, f_buf, f_col, f_z, f_y, prod, total, near_a, near_b, q_a, q_b, mt, pan,
    ay1, ay2, az1, az2, bz1, bz2, by1, by2,
    m1, m1r, m3, m5,
    s_sem, in_sem, u_sem, f_send, f_recv, f_local, fz_send, fz_recv, ucol_send, ucol_recv, rs_send, rs_recv, m_send, m_recv,
):
    r = lax.axis_index("row")
    c = lax.axis_index("col")
    x, core = r // 2, r % 2
    z, y = c // NY, c % NY
    root = c % NR
    quarter = c // NR
    is_root = root == r
    feeds = core == y % 2
    place = r * NY + y

    def near_dev(p):
        return (p // NY, z * NY + p % NY)

    def partner(u):
        side = z + 1 - 2 * (z % 2) if u // 2 else z
        return side * NY + (y + 2 * (u % 2)) % NY

    barrier = pltpu.get_barrier_semaphore()

    def greet(dev):
        pl.semaphore_signal(barrier, inc=1, device_id=dev, device_id_type=MESH)

    @pl.loop(0, 16)
    def _(m):
        @pl.when(jnp.logical_not(jnp.logical_and(is_root, 2 * m + core == c)))
        def _():
            greet((root, 2 * m + core))

    @pl.when(jnp.logical_and(feeds, jnp.logical_not(is_root)))
    def _():
        for u in range(TC):
            greet((root, partner(u)))

    xs = [((x + d) % NX) * 2 for d in range(NX)]
    ks = [core, 1 - core]
    ys = [(y + d) % NY for d in range(NY)]
    for dx in (2, 1, 3, 0):
        for dy in (2, 1, 3, 0):
            for dk in range(2):
                if dx or dk or dy:
                    greet((xs[dx] + ks[dk], z * NY + ys[dy]))

    @pl.loop(1, NZ)
    def _(d):
        greet((r, ((z + d) % NZ) * NY + y))

    s_copies = [
        pltpu.make_async_copy(s_hbm.at[pl.ds(t * 2048, 2048)], s_raw.at[t], s_sem.at[t])
        for t in range(TR)
    ]
    u_copy = pltpu.make_async_copy(u_hbm, u_row, u_sem)
    f_copy = pltpu.make_async_copy(f_hbm, f_own, in_sem.at[0])
    small = [
        pltpu.make_async_copy(c_hbm, c_ref, in_sem.at[1]),
        pltpu.make_async_copy(b_hbm, b_ref, in_sem.at[2]),
        pltpu.make_async_copy(pd_hbm, pd_ref, in_sem.at[3]),
    ]
    f_copy.start()
    for cp in s_copies[:2]:
        cp.start()
    u_copy.start()
    for cp in small:
        cp.start()
    for cp in s_copies[2:]:
        cp.start()

    f_copy.wait()
    f_wide = f_own[...].astype(F32)
    for q in range(4):
        f_parts[q] = jnp.concatenate(
            [f_wide[(4 * u + q) * 8 : (4 * u + q) * 8 + 8] for u in range(TC)], axis=0
        ).astype(BF16)

    for kind, store in (("A", f_z.at[z]), ("B", f_y.at[y])):
        for slot, g in enumerate(n for n, k in enumerate(KINDS) if k == kind):
            store[slot * 16 : slot * 16 + 16, :] = f_own[g * 16 : g * 16 + 16, :]

    def relay(t):
        s_f32[...] = s_raw[t].astype(F32)
        for u in range(TC):
            for half in range(2):
                s_rel[t, u, :, half * 128 : half * 128 + 128] = s_f32[
                    pl.ds(half * 4 + u, 256, stride=8), :
                ].astype(BF16)

    for t in range(EARLY):
        s_copies[t].wait()

    @pl.loop(0, EARLY)
    def _(t):
        relay(t)

    pl.semaphore_wait(barrier, 16 + 31 + 7 - jnp.where(is_root, 1, 0) + jnp.where(feeds, 3, 0))

    def rows_to(dq, dx):
        q = (z // 2 + dq) % 4
        return pltpu.make_async_remote_copy(
            src_ref=f_parts.at[q], dst_ref=f_buf.at[c % 2, c // 2],
            send_sem=f_send.at[NX * dq + dx], recv_sem=f_recv.at[0],
            device_id=(xs[dx] + c % 2, NR * q + r), device_id_type=MESH,
        )

    for dq in (2, 1, 3, 0):
        for dx in (2, 1, 3, 0):
            if dq or dx:
                rows_to(dq, dx).start()

    @pl.when(is_root)
    def _():
        pltpu.make_async_copy(f_parts.at[quarter], f_buf.at[c % 2, c // 2], f_recv.at[0]).start()

    @pl.when(jnp.logical_not(is_root))
    def _():
        rows_to(0, 0).start()

    def ucol_to(u, d):
        return pltpu.make_async_remote_copy(
            src_ref=u_hbm.at[u, quarter], dst_ref=u_col.at[u],
            send_sem=ucol_send.at[d], recv_sem=ucol_recv,
            device_id=(((x + d) % NX) * 2 + core, partner(u)), device_id_type=MESH,
        )

    def send_ucol():
        for u in range(TC):
            @pl.when(partner(u) % NR == r)
            def _():
                for d in (2, 1, 3):
                    ucol_to(u, d).start()

        @pl.when(is_root)
        def _():
            pltpu.make_async_copy(u_hbm.at[:, quarter], u_col, ucol_recv).start()

    send_ucol()

    def fz_to(rnd, way):
        sign = 1 if way == 0 else NZ - 1
        held = (z + (NZ - sign) * rnd) % NZ
        return pltpu.make_async_remote_copy(
            src_ref=f_z.at[held], dst_ref=f_z.at[held],
            send_sem=fz_send.at[4 * way + rnd], recv_sem=fz_recv.at[4 * way + rnd],
            device_id=(r, ((z + sign) % NZ) * NY + y), device_id_type=MESH,
        )

    def fy_to(d):
        return pltpu.make_async_remote_copy(
            src_ref=f_y.at[y], dst_ref=f_y.at[y],
            send_sem=fz_send.at[NZ + d], recv_sem=fz_recv.at[NZ + d],
            device_id=(r, z * NY + (y + d) % NY), device_id_type=MESH,
        )

    for t in range(EARLY, TR):
        s_copies[t].wait()

    @pl.loop(EARLY, TR)
    def _(t):
        relay(t)

    u_copy.wait()
    for cp in small:
        cp.wait()

    @pl.loop(0, TR)
    def _(t):
        rows = u_row[t // 4, t % 4].astype(F32)
        norm = jnp.sum(rows * rows, axis=-1, keepdims=True) * (2.0 * LOG2E / 256.0)
        norm_row[t] = jnp.broadcast_to(norm, (256, 128))

    panel = pd_ref[...].astype(F32)
    panel_norm = lax.dot_general(
        jnp.ones((8, 256), F32), panel * panel, (((1,), (1,)), ((), ())),
        precision=HIGHEST, preferred_element_type=F32,
    )

    def weights(rows):
        norm = jnp.sum(rows * rows, axis=-1, keepdims=True)
        cross = lax.dot_general(
            rows.astype(BF16), pd_ref[...], (((1,), (1,)), ((), ())), preferred_element_type=F32
        )
        scaled = (2.0 / 256.0) * (norm + panel_norm[0:1] - 2.0 * cross)
        weight = 2.0 * scaled * jnp.exp(-scaled) * (1.0 / math.sqrt(8388608))
        return lax.dot_general(
            weight, b_ref[...], (((1,), (1,)), ((), ())),
            precision=HIGHEST, preferred_element_type=F32,
        )

    group_slot = {}
    for g, kind in enumerate(KINDS):
        group_slot[g] = KINDS[:g].count(kind)
    pan[...] = jnp.zeros((8, 256), F32)
    for g, kind in enumerate(KINDS):
        slot = group_slot[g]
        rows = []
        if kind == "A":
            for zz in range(NZ):
                for t in range(g * PER, g * PER + PER):
                    first = pl.multiple_of(zz * 32 + (y // 2) * 16, 16)
                    pair = u_row[t // 4, t % 4, pl.ds(first, 16), :].astype(F32)
                    rows.append(jnp.where(y % 2 == 0, pair[0:8], pair[8:16]))
            near, mine = near_a, z
        else:
            wide = [
                u_row[t // 4, t % 4, pl.ds(pl.multiple_of(z * 32, 32), 32), :].astype(F32)
                for t in range(g * PER, g * PER + PER)
            ]
            for yy in range(NY):
                for w in wide:
                    rows.append(w[yy * 8 : yy * 8 + 8])
            near, mine = near_b, y
        near[slot] = weights(jnp.concatenate(rows, axis=0))
        own_c = c_ref[g * 16 : g * 16 + 16, :].astype(F32)
        own_w = near[slot, pl.ds(pl.multiple_of(mine * 16, 16), 16), :]
        pan[...] += jnp.sum((own_c * own_w).reshape(2, 8, 256), axis=0)
    mt[...] = lax.dot_general(
        f_own[...], c_ref[...], (((0,), (0,)), ((), ())), preferred_element_type=F32
    )

    sibling = (2 * x + 1 - core, c)

    pltpu.make_async_copy(f_buf.at[0], f_buf.at[0], f_recv.at[0]).wait()
    f_swap = pltpu.make_async_remote_copy(
        src_ref=f_buf.at[core], dst_ref=f_buf.at[core],
        send_sem=f_local, recv_sem=f_recv.at[1],
        device_id=sibling, device_id_type=MESH,
    )
    f_swap.start()

    f_swap.wait_recv()

    @pl.loop(0, 16, unroll=4)
    def _(m):
        even = f_buf[0, m].astype(F32)
        odd = f_buf[1, m].astype(F32)
        for u in range(TC):
            rows = jnp.concatenate([even[8 * u : 8 * u + 8], odd[8 * u : 8 * u + 8]], axis=0)
            f_col[u, pl.ds(pl.multiple_of(m * 16, 16), 16), :] = rows.astype(BF16)

    neighbours = {
        "y": ((r, z * NY + (y + 1) % NY), (r, z * NY + (y + NY - 1) % NY)),
        "z": ((r, ((z + 1) % NZ) * NY + y), (r, ((z + NZ - 1) % NZ) * NY + y)),
    }
    size = {"y": NY, "z": NZ}
    here = {"y": y, "z": z}
    lanes = (pl.ds(0, 128), pl.ds(128, 128))
    full = pl.ds(0, 256)
    def part(g, axis, dest, lane):
        rows = pl.ds(g * PER, PER)
        if KINDS[g] == "A":
            if axis == "y":
                return (rows, slice(None), dest, slice(None), lane)
            return (rows, dest, y, slice(None), lane)
        if axis == "z":
            return (rows, dest, slice(None), slice(None), lane)
        return (rows, z, dest, slice(None), lane)

    def box(g, axis, rnd, way):
        slot = group_slot[g]
        if KINDS[g] == "A":
            first, later = (ay1, ay2) if axis == "y" else (az1, az2)
        else:
            first, later = (bz1, bz2) if axis == "z" else (by1, by2)
        if rnd == 0:
            return first.at[slot, way]
        return later.at[slot, way, rnd - 1]

    def sem_of(g, axis, rnd, way):
        second = axis == ("z" if KINDS[g] == "A" else "y")
        offset = (size["y"] // 2 if KINDS[g] == "A" else size["z"] // 2) if second else 0
        return (g * 6 + offset + rnd) * 2 + way

    def copy_of(g, axis, rnd, way):
        n = size[axis]
        reach = n // 2 - rnd
        sign = 1 if way == 0 else n - 1
        dest = (here[axis] + sign * reach) % n
        lane = lanes[way] if rnd == 0 else full
        k = sem_of(g, axis, rnd, way)
        return pltpu.make_async_remote_copy(
            src_ref=prod.at[part(g, axis, dest, lane)],
            dst_ref=box(g, axis, rnd, way),
            send_sem=rs_send.at[k], recv_sem=rs_recv.at[k],
            device_id=neighbours[axis][way], device_id_type=MESH,
        )

    def take(g, axis, rnd, way):
        n = size[axis]
        reach = n // 2 - rnd - 1
        sign = 1 if way == 0 else n - 1
        dest = (here[axis] + sign * reach) % n
        lane = lanes[way] if rnd == 0 else full
        copy_of(g, axis, rnd, way).wait_recv()
        at = part(g, axis, dest, lane)
        prod[at] = prod[at] + box(g, axis, rnd, way)[...]

    def product(g):
        for t in range(g * PER, g * PER + PER):
            out = jnp.dot(s_rel[t, 0], f_col[0], preferred_element_type=F32)
            for u in range(1, TC):
                out += jnp.dot(s_rel[t, u], f_col[u], preferred_element_type=F32)
            prod[t] = out.reshape(NZ, NY, 8, 256)

    def keep_rows(g):
        slot = group_slot[g]
        span = range(g * PER, g * PER + PER)
        if KINDS[g] == "A":
            for n, piece in enumerate(prod[t, zz, y] for zz in range(NZ) for t in span):
                q_a[slot, n] = piece * (-2.0)
        else:
            for n, piece in enumerate(prod[t, z, yy] for yy in range(NY) for t in span):
                q_b[slot, n] = piece * (-2.0)

    def gather_moment(g):
        slot = group_slot[g]
        if KINDS[g] == "A":
            rows = q_a[slot].reshape(NZ * 16, 256)
            factor = f_z[:, slot * 16 : slot * 16 + 16, :].reshape(NZ * 16, 256)
            weight = near_a[slot]
        else:
            rows = q_b[slot].reshape(NY * 16, 256)
            factor = f_y[:, slot * 16 : slot * 16 + 16, :].reshape(NY * 16, 256)
            weight = near_b[slot]
        pan[...] += jnp.sum((rows * weight).reshape(-1, 8, 256), axis=0)
        flipped = jnp.transpose(factor.astype(F32)).astype(BF16)
        high = rows.astype(BF16)
        rest = rows - high.astype(F32)
        middle = rest.astype(BF16)
        low = (rest - middle.astype(F32)).astype(BF16)
        out = jnp.dot(flipped, low, preferred_element_type=F32)
        out += jnp.dot(flipped, middle, preferred_element_type=F32)
        out += jnp.dot(flipped, high, preferred_element_type=F32)
        mt[...] += out

    def step(g, k):
        axes = ("y", "z") if KINDS[g] == "A" else ("z", "y")
        first = size[axes[0]] // 2
        if k == 0:
            product(g)
            for way in range(2):
                copy_of(g, axes[0], 0, way).start()
            return
        for way in range(2):
            if k <= first:
                take(g, axes[0], k - 1, way)
                if k < first:
                    copy_of(g, axes[0], k, way).start()
            else:
                take(g, axes[1], k - first - 1, way)
                if k < STEPS - 1:
                    copy_of(g, axes[1], k - first, way).start()
        if k == first:
            for way in range(2):
                copy_of(g, axes[1], 0, way).start()
            keep_rows(g)

    def slope_row(t, acc):
        for u in range(TC):
            cross = lax.dot_general(
                u_row[t // 4, t % 4], u_col[u], (((1,), (1,)), ((), ())), preferred_element_type=F32
            )
            across = norm_col[u]
            for k in range(0, 256, 32):
                down = norm_row[t, k : k + 32]
                norms = jnp.concatenate([down, down], axis=1) + across[0:1]
                minus = cross[k : k + 32] * (4.0 * LOG2E / 256.0) - norms
                term = s_rel[t, u, k : k + 32].astype(F32) * (minus * jnp.exp2(minus))
                acc = acc + jnp.sum(term.reshape(4, 8, 256), axis=0)
        return acc

    def ucol_forward():
        return pltpu.make_async_remote_copy(
            src_ref=u_col, dst_ref=u_col,
            send_sem=ucol_send.at[0], recv_sem=ucol_recv,
            device_id=sibling, device_id_type=MESH,
        )

    n_groups = len(KINDS)

    def take_ucol():
        pltpu.make_async_copy(u_col, u_col, ucol_recv).wait()

        @pl.when(feeds)
        def _():
            ucol_forward().start()

        for u in range(TC):
            cols = u_col[u].astype(F32)
            norm = lax.dot_general(
                jnp.ones((8, 256), F32), cols * cols, (((1,), (1,)), ((), ())),
                precision=HIGHEST, preferred_element_type=F32,
            )
            norm_col[u] = norm * (2.0 * LOG2E / 256.0)

    def send_factors():
        for way in range(2):
            fz_to(0, way).start()

        @pl.loop(1, NY)
        def _(d):
            fy_to(d).start()

    def pass_factors(rnd):
        for way in range(2):
            fz_to(rnd - 1, way).wait_recv()
            if rnd + way < 4:
                fz_to(rnd, way).start()

    def take_factors():
        fz_to(3, 0).wait_recv()
        for d in range(1, NY):
            fy_to(d).wait_recv()

    near = []
    for dx in range(NX):
        for dk in range(2):
            for dy in range(NY):
                if dx or dk or dy:
                    near.append((min(dx, NX - dx) + min(dy, NY - dy) + 0.1 * dk, dx, dk, dy))
    near.sort(reverse=True)
    def to_near(stage, src, dst):
        out = []
        for _, dx, dk, dy in near:
            row = xs[dx] + ks[dk]
            out.append(pltpu.make_async_remote_copy(
                src_ref=src(row * NY + ys[dy]), dst_ref=dst,
                send_sem=m_send.at[stage], recv_sem=m_recv.at[stage],
                device_id=(row, z * NY + ys[dy]), device_id_type=MESH,
            ))
        return out

    copies1 = to_near(0, lambda p: m1.at[p], m1r.at[place])
    copies3 = to_near(2, lambda p: m5.at[place], m5.at[place])
    copies2 = [
        pltpu.make_async_remote_copy(
            src_ref=m3.at[z], dst_ref=m3.at[z],
            send_sem=m_send.at[1], recv_sem=m_recv.at[1],
            device_id=(r, ((z + d) % NZ) * NY + y), device_id_type=MESH,
        )
        for d in (4, 3, 5, 2, 6, 1, 7)
    ]

    def wait_all(ref, n, sem):
        blocks = ref.at[pl.ds(0, n)]
        pltpu.make_async_copy(blocks, blocks, sem).wait()

    def sum_first(acc):
        trail = jnp.sum(acc) * (-2.0 / LOG2E / 32768.0)
        panel_part = jnp.sum(pan[...])
        lane = lax.broadcasted_iota(jnp.int32, (8, 256), 1)
        down = lax.broadcasted_iota(jnp.int32, (8, 256), 0)
        for p in range(NR * NY):
            block = jnp.where(jnp.logical_and(down == 7, lane == 0), trail, mt[8 * p : 8 * p + 8])
            m1[p] = jnp.where(jnp.logical_and(down == 7, lane == 1), panel_part, block)
        m1r[place] = m1[place]
        for cp in copies1:
            cp.start()

    def sum_second():
        wait_all(m1r, NR * NY - 1, m_recv.at[0])
        part = m1r[0]
        for j in range(1, NR * NY):
            part = part + m1r[j]
        m3[z] = part
        for cp in copies2:
            cp.start()

    def sum_third():
        wait_all(m3, NZ - 1, m_recv.at[1])
        part = m3[0]
        for j in range(1, NZ):
            part = part + m3[j]
        m5[place] = part
        for cp in copies3:
            cp.start()
        slope_ref[...] = part[7:8, 0:2]

    acc = jnp.zeros((8, 256), F32)
    done = 0
    for event in SCHEDULE:
        if event[0] == "step":
            step(event[1], event[2])
        elif event[0] == "slope":
            acc = lax.fori_loop(done, done + event[1], slope_row, acc)
            done += event[1]
        elif event[0] == "ucol":
            take_ucol()
        elif event[0] == "send":
            send_factors()
        elif event[0] == "pass":
            pass_factors(event[1])
        elif event[0] == "moment":
            gather_moment(event[1])
        elif event[0] == "factors":
            take_factors()
        elif event[0] == "sum1":
            sum_first(acc)
        elif event[0] == "sum2":
            sum_second()

    sum_third()

    for t in range(TR):
        total[pl.ds(t * 8, 8), :] = (
            c_ref[pl.ds((t // 2) * 16, 16), :].astype(F32)[(t % 2) * 8 : (t % 2) * 8 + 8]
            - 2.0 * prod[t, z, y]
        )
    adj_ref[...] = jnp.dot(total[...], b_ref[...], precision=HIGHEST, preferred_element_type=F32)
    adj_copy = pltpu.make_async_copy(adj_ref, adj_hbm, in_sem.at[4])
    adj_copy.start()

    adj_copy.wait()
    wait_all(m1r, NR * NY - 1, m_send.at[0])
    wait_all(m3, NZ - 1, m_send.at[1])
    for dq in range(4):
        for dx in range(NX):
            if dq or dx:
                rows_to(dq, dx).wait_send()

    @pl.when(jnp.logical_not(is_root))
    def _():
        rows_to(0, 0).wait_send()

    @pl.when(feeds)
    def _():
        for d in (1, 2, 3):
            ucol_to(0, d).wait_send()
        ucol_forward().wait_send()

    f_swap.wait_send()
    for rnd in range(4):
        for way in range(2):
            if rnd + way < 4:
                fz_to(rnd, way).wait_send()
    for d in range(1, NY):
        fy_to(d).wait_send()
    for g, kind in enumerate(KINDS):
        for axis in "yz":
            for rnd in range(size[axis] // 2):
                for way in range(2):
                    copy_of(g, axis, rnd, way).wait_send()

    wait_all(m5, NR * NY - 1, m_recv.at[2])
    moment_ref[...] = m5[...]
    wait_all(m5, NR * NY - 1, m_send.at[2])

def finish(adj_in, m_in, slope_in, b_ref, adj_ref, diag_ref, slope_ref):
    adj_ref[...] = adj_in[...]
    slope_ref[...] = slope_in[...]
    diag = lax.dot_general(
        b_ref[...], m_in[...], (((0,), (1,)), ((), ())),
        precision=HIGHEST, preferred_element_type=F32,
    )
    down = lax.broadcasted_iota(jnp.int32, (256, 256), 0)
    across = lax.broadcasted_iota(jnp.int32, (256, 256), 1)
    diag_ref[...] = jnp.where(down >= across, -diag, 0.0)


def local(trailing_cot, panel_factor, panel_cot, block_inverse, row_desc, panel_desc):
    s_rows = trailing_cot.reshape(TR, 256, TC, 2, 128).transpose(0, 1, 3, 2, 4).reshape(TR * 2048, 128)
    hbm = pl.BlockSpec(memory_space=pl.ANY)
    vmem = pl.BlockSpec(memory_space=pltpu.VMEM)
    dma = pltpu.SemaphoreType.DMA
    V = pltpu.VMEM
    adjoint, moment, slope = pl.pallas_call(
        kernel,
        out_shape=(
            jax.ShapeDtypeStruct((128, 256), F32),
            jax.ShapeDtypeStruct((NR * NY, 8, 256), F32),
            jax.ShapeDtypeStruct((1, 2), F32),
        ),
        in_specs=[hbm] * 6,
        out_specs=(hbm, vmem, vmem),
        scratch_shapes=[
            V((128, 256), BF16),
            V((128, 256), BF16),
            V((256, 256), F32),
            V((256, 256), BF16),
            V((128, 256), F32),
            V((TR, 2048, 128), BF16),
            V((2048, 128), F32),
            V((TR, TC, 256, 256), BF16),
            V((4, 4, 256, 256), BF16),
            V((TC, 256, 256), BF16),
            V((TR, 256, 128), F32),
            V((TC, 8, 256), F32),
            V((4, 32, 256), BF16),
            V((2, 16, 32, 256), BF16),
            V((TC, 256, 256), BF16),
            V((NZ, N_A * 16, 256), BF16),
            V((NY, N_B * 16, 256), BF16),
            V((TR, NZ, NY, 8, 256), F32),
            V((128, 256), F32),
            V((N_A, NZ * 16, 256), F32),
            V((N_B, NY * 16, 256), F32),
            V((N_A, NZ * 2, 8, 256), F32),
            V((N_B, NY * 2, 8, 256), F32),
            V((256, 256), F32),
            V((8, 256), F32),
            V((N_A, 2, PER, NZ, 8, 128), F32),
            V((N_A, 2, 1, PER, NZ, 8, 256), F32),
            V((N_A, 2, PER, 8, 128), F32),
            V((N_A, 2, 3, PER, 8, 256), F32),
            V((N_B, 2, PER, NY, 8, 128), F32),
            V((N_B, 2, 3, PER, NY, 8, 256), F32),
            V((N_B, 2, PER, 8, 128), F32),
            V((N_B, 2, 1, PER, 8, 256), F32),
            V((NR * NY, 8, 256), F32),
            V((NR * NY, 8, 256), F32),
            V((NZ, 8, 256), F32),
            V((NR * NY, 8, 256), F32),
            dma((TR,)),
            dma((5,)),
            dma,
            dma((16,)),
            dma((2,)),
            dma,
            dma((NZ + NY,)),
            dma((NZ + NY,)),
            dma((4,)),
            dma,
            dma((len(KINDS) * 12,)),
            dma((len(KINDS) * 12,)),
            dma((3,)),
            dma((3,)),
        ],
        compiler_params=pltpu.CompilerParams(
            collective_id=0, has_side_effects=True, vmem_limit_bytes=60 * 1024 * 1024
        ),
        cost_estimate=pl.CostEstimate(
            flops=4 * 4096 * 1024 * 256, bytes_accessed=12 * 1024 * 1024, transcendentals=4096 * 1024
        ),
        name="panel_step",
    )(
        row_desc.reshape(4, 4, 256, 256),
        s_rows,
        panel_cot.reshape(128, 256),
        panel_factor.reshape(128, 256),
        block_inverse,
        panel_desc,
    )
    adjoint, diag, slope = pl.pallas_call(
        finish,
        out_shape=(
            jax.ShapeDtypeStruct((128, 256), F32),
            jax.ShapeDtypeStruct((256, 256), F32),
            jax.ShapeDtypeStruct((1, 2), F32),
        ),
        in_specs=[vmem] * 4,
        out_specs=(vmem, vmem, vmem),
        name="finish",
    )(adjoint, moment.reshape(256, 256), slope, block_inverse)
    return adjoint.reshape(16, 8, 256), diag, slope.reshape(2)


def solution(mesh):
    in_specs = (
        P(None, "row", None, "col"),
        P(None, ("row", "col"), None),
        P(None, ("row", "col"), None),
        P(),
        P(None, "row", None),
        P(),
    )
    out_specs = (P(None, ("row", "col"), None), P(), P())
    return jax.shard_map(local, mesh=mesh, in_specs=in_specs, out_specs=out_specs, check_vma=False)
```
